256 devices in a mesh: dp: 4 (over x), vocab: 64 (over y, z, core).
Axes of the slice: x: 4, y: 4, z: 8, core: 2. Of those that a mesh axis runs over, the one named last changes fastest.
Arguments:
- student_hidden: bfloat16 [2048, 2560], P(('dp', 'vocab')), parts along dimension 0, may hold values from -48.620019 to 48.620019
- teacher_hidden: bfloat16 [2048, 2048], P(('dp', 'vocab')), parts along dimension 0, may hold values from -54.358834 to 54.358834
- student_head: bfloat16 [10240, 81920], P('dp', 'vocab'), parts along dimension 0, may hold values from -0.118585412 to 0.118585412
- teacher_head: bfloat16 [8192, 81920], P('dp', 'vocab'), parts along dimension 0, may hold values from -0.13258252 to 0.13258252
- segment_ids: int32 [2048], P('dp'), parts along dimension 0, may hold values from 0 to 15, as said below
- valid_mask: int32 [2048], P('dp'), parts along dimension 0, may hold values from 0 to 1
Outputs:
- token_kl: float32 [2048], P(('dp', 'vocab')), parts along dimension 0
- hidden_grad: bfloat16 [2048, 2560], P(('dp', 'vocab')), parts along dimension 0
The draws below stay inside these ranges and needn't reach their ends.
There are 4 independent parts, one for each index of `dp`. The reference program is written for one: setup_inputs(seed, part) draws one part's arguments, and reference() takes and returns one part's arrays. A program takes and returns all parts, laid end to end along the dimension named above; each array names one. Nothing has to cross between parts.
Inputs may be any that keep to these rules, and one draw needn't show every extreme that they name: `segment_ids`: ids never fall; each packed sequence holds 16 to 48 tokens, one exactly 48.
All inputs are finite; a program needn't handle non-finite values.
Results may differ from the reference program's by a relative error of at most 0.005.
Values may be sent and summed in bfloat16 or wider, within the bound.
A program may use at most 64 MiB of HBM per device.

```python
import jax
import jax.numpy as jnp
from jax import lax

HS = 2560
HT = 2048
TOKENS = 512
SEGS = 16
VOCAB = 81920


def packing(key):
    key = jax.random.fold_in(key, 41)
    half_count = SEGS // 2
    spread = jax.random.randint(jax.random.fold_in(key, 1), (half_count,), 0, 17).astype(jnp.int32)
    spread = spread.at[0].set(16)
    lengths = jnp.concatenate([32 + spread, 32 - spread]).astype(jnp.int32)
    order = jax.random.permutation(jax.random.fold_in(key, 2), SEGS)
    lengths = lengths[order]
    ends = jnp.cumsum(lengths).astype(jnp.int32)
    positions = jnp.arange(TOKENS, dtype=jnp.int32)
    passed = (positions[:, None] >= ends[None, :SEGS - 1]).astype(jnp.int32)
    return jnp.sum(passed, axis=1).astype(jnp.int32)


def draw_segment_ids(key, part):
    return packing(key)


def draw_valid_mask(key, part):
    seg_of_token = packing(key)
    key = jax.random.fold_in(key, 52)
    silent_seg = jax.random.randint(jax.random.fold_in(key, 1), (), 0, SEGS).astype(jnp.int32)
    coins = jax.random.randint(jax.random.fold_in(key, 2), (TOKENS,), 0, 4).astype(jnp.int32)
    keep = jnp.logical_and(coins > 0, seg_of_token != silent_seg)
    return jnp.where(keep, 1, 0).astype(jnp.int32)


def draw_student_head(key, part):
    key = jax.random.fold_in(key, 21)
    base = jnp.clip(jax.random.normal(key, (HS, VOCAB), jnp.float32), -6.0, 6.0) * HS ** (-0.5)
    return base.astype(jnp.bfloat16)


def draw_teacher_head(key, part):
    key = jax.random.fold_in(key, 22)
    base = jnp.clip(jax.random.normal(key, (HT, VOCAB), jnp.float32), -6.0, 6.0) * HT ** (-0.5)
    return base.astype(jnp.bfloat16)


def draw_student_hidden(key, part):
    key = jax.random.fold_in(key, 31)
    base = jnp.clip(jax.random.normal(key, (TOKENS, HS), jnp.float32), -6.0, 6.0) * 3.0
    return base.astype(jnp.bfloat16)


def draw_teacher_hidden(key, part):
    key = jax.random.fold_in(key, 32)
    base = jnp.clip(jax.random.normal(key, (TOKENS, HT), jnp.float32), -6.0, 6.0) * 3.0
    return base.astype(jnp.bfloat16)


def setup_inputs(seed: int = 0, part: int = 0) -> dict:
    splits = jax.random.split(jax.random.key(seed), 7)
    own_keys = jax.random.split(jax.random.fold_in(splits[6], part), 7)
    student_hidden = draw_student_hidden(jax.random.fold_in(jax.random.fold_in(splits[6], part), 71), part)
    teacher_hidden = draw_teacher_hidden(jax.random.fold_in(jax.random.fold_in(splits[6], part), 71), part)
    student_head = draw_student_head(jax.random.fold_in(jax.random.fold_in(splits[6], part), 71), part)
    teacher_head = draw_teacher_head(jax.random.fold_in(jax.random.fold_in(splits[6], part), 71), part)
    segment_ids = draw_segment_ids(jax.random.fold_in(jax.random.fold_in(splits[6], part), 71), part)
    valid_mask = draw_valid_mask(jax.random.fold_in(jax.random.fold_in(splits[6], part), 71), part)
    return dict(student_hidden=student_hidden, teacher_hidden=teacher_hidden, student_head=student_head, teacher_head=teacher_head, segment_ids=segment_ids, valid_mask=valid_mask)


LOSS_SCALE = 1024.0


def reference(student_hidden, teacher_hidden, student_head, teacher_head, segment_ids, valid_mask):
    student_logits = jnp.dot(student_hidden, student_head, preferred_element_type=jnp.float32)
    teacher_logits = jnp.dot(teacher_hidden, teacher_head, preferred_element_type=jnp.float32)
    log_ratio = student_logits - teacher_logits
    peak_student = jnp.max(student_logits, axis=1, keepdims=True)
    peak_teacher = jnp.max(teacher_logits, axis=1, keepdims=True)
    student_exp = jnp.exp(student_logits - peak_student)
    sum_student = jnp.sum(student_exp, axis=1)
    sum_teacher = jnp.sum(jnp.exp(teacher_logits - peak_teacher), axis=1)
    cross = jnp.sum(student_exp * log_ratio, axis=1)
    lse_student = peak_student[:, 0] + jnp.log(sum_student)
    lse_teacher = peak_teacher[:, 0] + jnp.log(sum_teacher)
    token_kl = cross / sum_student - lse_student + lse_teacher
    member = (segment_ids[:, None] == jnp.arange(SEGS, dtype=jnp.int32)[None, :]).astype(jnp.float32)
    valid = valid_mask.astype(jnp.float32)
    counts = jnp.sum(member * valid[:, None], axis=0)
    row_count = jnp.sum(member * counts[None, :], axis=1)
    weight = LOSS_SCALE * valid / jnp.maximum(row_count, 1.0)
    offset = lse_student - lse_teacher + token_kl
    grad_logits = (weight[:, None] * jnp.exp(student_logits - lse_student[:, None])
                   * (log_ratio - offset[:, None])).astype(jnp.bfloat16)
    hidden_grad = lax.dot_general(grad_logits, student_head, (((1,), (1,)), ((), ())),
                                  preferred_element_type=jnp.float32)
    return token_kl, hidden_grad.astype(jnp.bfloat16)
```

```python
import functools

import jax
import jax.numpy as jnp
from jax import lax
from jax.experimental import pallas as pl
from jax.experimental.pallas import tpu as pltpu
from jax.sharding import PartitionSpec as P

LOSS_SCALE = 1024.0
NY, NZ, NC = 4, 8, 2
HZ = NZ // 2
BLK = 16
HALF = NY * HZ * BLK
TILE = 256
MESH = pl.DeviceIdType.MESH


def kernel(
    hs, ht, vs,
    sh_ref, th_ref, seg_ref, valid_ref, ws_hbm, wt_hbm,
    kl_ref, out_ref,
    ws, wt, x, xf, xg, logit_s, logit_t,
    stat_col, stat_own, stat_z, stat_mid, stat_y, fac, wcol,
    ps, pr, r1, ra, r2a, ra2, rb, r2b, rb2, fin, fin_in,
    load_sem, pair_s, pair_r,
    a1_s, a1_r, a2_s, a2_r, b1_s, b1_r, b2_s, b2_r, sib_s, sib_r,
    sz_s, sz_r, sy_s, sy_r, ps_s, ps_r,
    ra1_s, ra1_r, ra2_s, ra2_r, rb1_s, rb1_r, rb2_s, rb2_r, fin_s, fin_r,
):
    v = lax.axis_index("vocab")
    y, z, c = v // (NZ * NC), (v // NC) % NZ, v % NC
    zz, par = z // 2, z % 2
    hs2, ht2 = hs // 2, ht // 2
    sa, ta = (hs2 * 4 // 5) // 128 * 128, (ht2 * 3 // 4) // 128 * 128
    widths = ((sa, hs2 - sa), (ta, ht2 - ta))

    def dev(dy, dz, dc):
        return {"vocab": (((y + dy) % NY) * NZ + (z + dz) % NZ) * NC + (c + dc) % NC}

    def rcopy(src, dst, ssem, rsem, device):
        return pltpu.make_async_remote_copy(
            src_ref=src, dst_ref=dst, send_sem=ssem, recv_sem=rsem,
            device_id=device, device_id_type=MESH,
        )

    load_s = pltpu.make_async_copy(ws_hbm, ws, load_sem.at[0])
    load_t = pltpu.make_async_copy(wt_hbm, wt, load_sem.at[1])
    load_s.start()
    load_t.start()

    barrier = pltpu.get_barrier_semaphore()
    partners = [(0, k, 0) for k in range(1, NZ)]
    partners += [(j, 0, d) for j in range(1, NY) for d in range(NC)] + [(0, 0, 1)]
    for p in partners:
        pl.semaphore_signal(barrier, inc=1, device_id=dev(*p), device_id_type=MESH)
    xf[:, :hs2] = sh_ref[:, pl.ds(pl.multiple_of((1 - c) * hs2, 128), hs2)].astype(jnp.float32)
    xf[:, hs2:] = th_ref[:, pl.ds(pl.multiple_of((1 - c) * ht2, 128), ht2)].astype(jnp.float32)
    pl.semaphore_wait(barrier, len(partners))
    pair = rcopy(xf, xg, pair_s, pair_r, dev(0, 0, 1))
    pair.start()

    seg = jnp.broadcast_to(seg_ref[...].astype(jnp.float32), (128, 2 * HALF))
    val = jnp.broadcast_to(valid_ref[...].astype(jnp.float32), (128, 2 * HALF))
    seg_c, val_c = jnp.transpose(seg)[:, :1], jnp.transpose(val)[:, :1]
    same = jnp.where(seg_c == seg[:1, :], val[:1, :], 0.0)
    count = jnp.sum(same, axis=1, keepdims=True)
    weight = LOSS_SCALE * val_c / jnp.maximum(count, 1.0)
    wcol[...] = jnp.broadcast_to(weight, (2 * HALF, 128)).reshape(NY, HZ, 2, BLK, 128)

    pair.wait()

    def put(col, width, full, part):
        mine = full[:, pl.ds(pl.multiple_of(c * width, 128), width)].astype(jnp.float32)
        both = jnp.concatenate(
            [jnp.where(c == 0, mine, part), jnp.where(c == 0, part, mine)], axis=0
        )
        x[par, y, zz, :, pl.ds(pl.multiple_of(col + c * width, 128), width)] = both.astype(
            jnp.bfloat16
        )

    put(0, hs2, sh_ref, xg[:, :hs2])
    put(hs, ht2, th_ref, xg[:, hs2:])

    def cols(u, order, core):
        start = (core * hs2, hs + core * ht2)[u] + (0 if order == 0 else widths[u][0])
        return pl.ds(pl.multiple_of(start, 128), widths[u][order])

    def span(u, core):
        start, width = ((core * hs2, hs2), (hs + core * ht2, ht2))[u]
        return pl.ds(pl.multiple_of(start, 128), width)

    def loop(lo, hi, body):
        def step(i, carry):
            body(i)
            return carry

        lax.fori_loop(lo, hi, step, 0)

    def a1(h, u, k):
        block = x.at[h, y, zz, :, cols(u, 0, c)]
        return rcopy(block, block, a1_s.at[h, u, k], a1_r.at[h, u, k], dev(0, k, 0))

    def a1_in(h, u, k):
        block = x.at[h, y, ((z - k) % NZ) // 2, :, cols(u, 0, c)]
        return rcopy(block, block, a1_s.at[h, u, k], a1_r.at[h, u, k], dev(0, k, 0))

    def a2(h, u, j):
        block = x.at[h, y, :, :, cols(u, 0, c)]
        return rcopy(block, block, a2_s.at[h, u, j], a2_r.at[h, u, j], dev(j, 0, 0))

    def a2_in(h, u, j):
        block = x.at[h, (y - j) % NY, :, :, cols(u, 0, c)]
        return rcopy(block, block, a2_s.at[h, u, j], a2_r.at[h, u, j], dev(j, 0, 0))

    def b1(h, u, j):
        block = x.at[h, y, zz, :, cols(u, 1, c)]
        return rcopy(block, block, b1_s.at[h, u, j], b1_r.at[h, u, j], dev(j, 0, 0))

    def b1_in(h, u, j):
        block = x.at[h, (y - j) % NY, zz, :, cols(u, 1, c)]
        return rcopy(block, block, b1_s.at[h, u, j], b1_r.at[h, u, j], dev(j, 0, 0))

    def b2(h, u, k):
        block = x.at[h, :, zz, :, cols(u, 1, c)]
        return rcopy(block, block, b2_s.at[h, u, k], b2_r.at[h, u, k], dev(0, k, 0))

    def b2_in(h, u, k):
        block = x.at[h, :, ((z - k) % NZ) // 2, :, cols(u, 1, c)]
        return rcopy(block, block, b2_s.at[h, u, k], b2_r.at[h, u, k], dev(0, k, 0))

    def sib(h, u, core):
        block = x.at[h, :, :, :, span(u, core)]
        return rcopy(block, block, sib_s.at[h, u], sib_r.at[h, u], dev(0, 0, 1))

    def from_parity(h, body):
        first = jnp.where(par == h, 2, 1)
        count = jnp.where(par == h, HZ - 1, HZ)
        loop(0, count, lambda i: body(first + 2 * i))

    def send_first(h, u):
        @pl.when(par == h)
        def _():
            loop(1, NZ, lambda k: a1(h, u, k).start())
            loop(1, NY, lambda j: b1(h, u, j).start())

    def send_second(h, u):
        from_parity(h, lambda k: a1_in(h, u, k).wait_recv())
        loop(1, NY, lambda j: a2(h, u, j).start())

        @pl.when(par == h)
        def _():
            loop(1, NY, lambda j: b1_in(h, u, j).wait_recv())
            loop(1, NZ, lambda k: b2(h, u, k).start())

    def send_sibling(h, u):
        loop(1, NY, lambda j: a2_in(h, u, j).wait_recv())
        from_parity(h, lambda k: b2_in(h, u, k).wait_recv())
        sib(h, u, c).start()

    def student(h):
        sib(h, 0, 1 - c).wait_recv()
        rows = x[h, :, :, :, :hs].reshape(HALF, hs)

        def tile(i):
            at = pl.ds(pl.multiple_of(i * TILE, TILE), TILE)
            logit_s[h, :, at] = jnp.dot(rows, ws[:, at], preferred_element_type=jnp.float32)

        loop(0, vs // TILE, tile)

    def teacher(h):
        sib(h, 1, 1 - c).wait_recv()
        rows = x[h, :, :, :, hs:].reshape(HALF, ht)

        def tile(i):
            at = pl.ds(pl.multiple_of(i * TILE, TILE), TILE)
            logit_t[h, :, at] = jnp.dot(rows, wt[:, at], preferred_element_type=jnp.float32)

        loop(0, vs // TILE, tile)

    lane = lax.broadcasted_iota(jnp.int32, (1, 128), 1)

    def stats(h):
        def part(i):
            at = pl.ds(pl.multiple_of(i * 32, 32), 32)
            s, t = logit_s[h, at, :], logit_t[h, at, :]
            peak_s = jnp.max(s, axis=1, keepdims=True)
            peak_t = jnp.max(t, axis=1, keepdims=True)
            e = jnp.exp(s - peak_s)
            ratio = s - t
            logit_s[h, at, :] = e
            logit_t[h, at, :] = ratio
            sum_s = jnp.sum(e, axis=1, keepdims=True)
            cross = jnp.sum(e * ratio, axis=1, keepdims=True)
            sum_t = jnp.sum(jnp.exp(t - peak_t), axis=1, keepdims=True)
            packed = jnp.where(lane == 0, peak_s, 0.0)
            for n, value in enumerate((sum_s, cross, peak_t, sum_t)):
                packed = jnp.where(lane == n + 1, value, packed)
            stat_col[h, at, :] = packed

        loop(0, HALF // 32, part)
        stat_own[h] = jnp.transpose(stat_col[h])[:8, :]

    def sz(h, k):
        return rcopy(stat_own.at[h], stat_z.at[h, k], sz_s.at[h, k], sz_r.at[h, k], dev(0, k, 0))

    def sy(h, n):
        j, d = n // NC, n % NC
        return rcopy(stat_mid.at[h], stat_y.at[h, n], sy_s.at[h, n], sy_r.at[h, n], dev(j, 0, d))

    def merge(blocks):
        peak_s = functools.reduce(jnp.maximum, [b[0:1] for b in blocks])
        peak_t = functools.reduce(jnp.maximum, [b[3:4] for b in blocks])
        sum_s = cross = sum_t = 0.0
        for b in blocks:
            scale = jnp.exp(b[0:1] - peak_s)
            sum_s = sum_s + scale * b[1:2]
            cross = cross + scale * b[2:3]
            sum_t = sum_t + jnp.exp(b[3:4] - peak_t) * b[4:5]
        return peak_s, sum_s, cross, peak_t, sum_t

    def stats_z(h):
        loop(1, NZ, lambda k: sz(h, k).start())

    def stats_y(h):
        loop(1, NZ, lambda k: sz(h, k).wait_recv())
        rows = merge([stat_own[h]] + [stat_z[h, k] for k in range(1, NZ)])
        stat_mid[h] = jnp.concatenate(list(rows) + [jnp.zeros((3, HALF), jnp.float32)], axis=0)
        loop(1, NY * NC, lambda n: sy(h, n).start())

    def factors(h):
        loop(1, NY * NC, lambda n: sy(h, n).wait_recv())
        peak_s, sum_s, cross, peak_t, sum_t = merge(
            [stat_mid[h]] + [stat_y[h, n] for n in range(1, NY * NC)]
        )
        lse_s, lse_t = peak_s + jnp.log(sum_s), peak_t + jnp.log(sum_t)
        kl = cross / sum_s - lse_s + lse_t
        offset = lse_s - lse_t + kl
        scale = jnp.exp(stat_own[h][0:1] - lse_s)
        packed = jnp.concatenate(
            [scale, offset, kl, jnp.zeros((125, HALF), jnp.float32)], axis=0
        )
        fac[h] = jnp.transpose(packed)

    def grad_rows(h):
        w = wcol[:, :, h, :, 0:1].reshape(HALF, 1)
        scale, offset = fac[h, :, 0:1] * w, fac[h, :, 1:2]
        return (scale * logit_s[h] * (logit_t[h] - offset)).astype(jnp.bfloat16)

    def back(h, grad, core, i):
        at = pl.ds(pl.multiple_of(core * hs2 + i * (hs2 // 2), 128), hs2 // 2)
        return lax.dot_general(
            grad, ws[at, :], (((1,), (1,)), ((), ())), preferred_element_type=jnp.float32
        )

    def swap(h):
        return rcopy(ps.at[h], pr.at[h], ps_s.at[h], ps_r.at[h], dev(0, 0, 1))

    def ra1(h, j):
        return rcopy(
            r1.at[h, (y + j) % NY, :, :, pl.ds(0, sa)], ra.at[h, j],
            ra1_s.at[h, j], ra1_r.at[h, j], dev(j, 0, 0),
        )

    def rb1(h, k):
        return rcopy(
            r1.at[h, :, ((z + k) % NZ) // 2, :, pl.ds(sa, hs2 - sa)], rb.at[h, k],
            rb1_s.at[h, k], rb1_r.at[h, k], dev(0, k, 0),
        )

    def rra2(h, k):
        return rcopy(
            r2a.at[h, ((z + k) % NZ) // 2], ra2.at[h, k],
            ra2_s.at[h, k], ra2_r.at[h, k], dev(0, k, 0),
        )

    def rrb2(h, j):
        return rcopy(
            r2b.at[h, (y + j) % NY], rb2.at[h, j],
            rb2_s.at[h, j], rb2_r.at[h, j], dev(j, 0, 0),
        )

    def to_parity(h, body):
        from_parity(h, body)

    def backward(h):
        grad = grad_rows(h)
        width = hs2 // 2

        for i in range(2):
            ps[h, :, i * width:(i + 1) * width] = back(h, grad, 1 - c, i)
        swap(h).start()
        for i in range(2):
            pr_at = slice(i * width, (i + 1) * width)
            fin[:, :, :, pr_at] = back(h, grad, c, i).reshape(NY, HZ, BLK, width)
        swap(h).wait_recv()
        total = fin[...] + pr[h].reshape(NY, HZ, BLK, hs2)
        r1[h] = total.astype(jnp.bfloat16)
        loop(1, NY, lambda j: ra1(h, j).start())
        to_parity(h, lambda k: rb1(h, k).start())

    def reduce_second(h):
        loop(1, NY, lambda j: ra1(h, j).wait_recv())
        total = r1[h, y, :, :, :sa].astype(jnp.float32)
        for j in range(1, NY):
            total = total + ra[h, j].astype(jnp.float32)
        r2a[h] = total.astype(jnp.bfloat16)
        to_parity(h, lambda k: rra2(h, k).start())

        @pl.when(par == h)
        def _():
            loop(1, NZ, lambda k: rb1(h, k).wait_recv())
            total = r1[h, :, zz, :, sa:].astype(jnp.float32)
            for k in range(1, NZ):
                total = total + rb[h, k].astype(jnp.float32)
            r2b[h] = total.astype(jnp.bfloat16)
            loop(1, NY, lambda j: rrb2(h, j).start())

    def final(h):
        @pl.when(par == h)
        def _():
            loop(1, NZ, lambda k: rra2(h, k).wait_recv())
            loop(1, NY, lambda j: rrb2(h, j).wait_recv())
            left = r2a[h, zz].astype(jnp.float32)
            for k in range(1, NZ):
                left = left + ra2[h, k].astype(jnp.float32)
            right = r2b[h, y].astype(jnp.float32)
            for j in range(1, NY):
                right = right + rb2[h, j].astype(jnp.float32)
            fin[0, 0, :, :sa] = left
            fin[0, 0, :, sa:] = right
            give = rcopy(
                fin.at[0, 0, pl.ds(pl.multiple_of((1 - c) * 8, 8), 8), :], fin_in,
                fin_s, fin_r, dev(0, 0, 1),
            )
            give.start()
            mine = pl.ds(pl.multiple_of(c * hs2, 128), hs2)
            theirs = pl.ds(pl.multiple_of((1 - c) * hs2, 128), hs2)
            out_ref[:, mine] = fin[0, 0, pl.ds(pl.multiple_of(c * 8, 8), 8), :]
            at = pl.multiple_of((y * HZ + zz) * BLK + c * 8, 8)
            kl_ref[...] = fac[h, pl.ds(at, 8), :]
            give.wait()
            out_ref[:, theirs] = fin_in[...]

    send_first(0, 0)
    send_first(0, 1)
    send_second(0, 0)
    send_first(1, 0)
    send_second(0, 1)
    send_first(1, 1)
    send_second(1, 0)
    send_sibling(0, 0)
    load_s.wait()
    student(0)
    send_second(1, 1)
    send_sibling(0, 1)
    load_t.wait()
    teacher(0)
    stats(0)
    stats_z(0)
    send_sibling(1, 0)
    student(1)
    stats_y(0)
    send_sibling(1, 1)
    teacher(1)
    stats(1)
    stats_z(1)
    factors(0)
    backward(0)
    stats_y(1)
    reduce_second(0)
    factors(1)
    backward(1)
    reduce_second(1)
    final(0)
    final(1)

    for h in range(2):
        for u in range(2):
            @pl.when(par == h)
            def _():
                loop(1, NZ, lambda k: a1(h, u, k).wait_send())
                loop(1, NY, lambda j: b1(h, u, j).wait_send())
                loop(1, NZ, lambda k: b2(h, u, k).wait_send())

            loop(1, NY, lambda j: a2(h, u, j).wait_send())
            sib(h, u, c).wait_send()
        loop(1, NZ, lambda k: sz(h, k).wait_send())
        loop(1, NY * NC, lambda n: sy(h, n).wait_send())
        swap(h).wait_send()
        loop(1, NY, lambda j: ra1(h, j).wait_send())
        to_parity(h, lambda k: rb1(h, k).wait_send())
        to_parity(h, lambda k: rra2(h, k).wait_send())

        @pl.when(par == h)
        def _():
            loop(1, NY, lambda j: rrb2(h, j).wait_send())


def local(student_hidden, teacher_hidden, student_head, teacher_head, segment_ids, valid_mask):
    rows, hs = student_hidden.shape
    ht = teacher_hidden.shape[1]
    vs = student_head.shape[1]
    tokens = segment_ids.shape[0]
    hs2 = hs // 2
    sa = (hs2 * 4 // 5) // 128 * 128
    f32, bf16 = jnp.float32, jnp.bfloat16
    dma = pltpu.SemaphoreType.DMA
    vmem = pl.BlockSpec(memory_space=pltpu.VMEM)
    hbm = pl.BlockSpec(memory_space=pl.ANY)
    flops = 2 * tokens * vs * (2 * hs + ht)
    kl, grad = pl.pallas_call(
        functools.partial(kernel, hs, ht, vs),
        out_shape=(
            jax.ShapeDtypeStruct((rows, 128), f32),
            jax.ShapeDtypeStruct((rows, hs), f32),
        ),
        in_specs=[vmem, vmem, vmem, vmem, hbm, hbm],
        out_specs=(vmem, vmem),
        scratch_shapes=[
            pltpu.VMEM((hs, vs), bf16),
            pltpu.VMEM((ht, vs), bf16),
            pltpu.VMEM((2, NY, HZ, BLK, hs + ht), bf16),
            pltpu.VMEM((rows, (hs + ht) // 2), f32),
            pltpu.VMEM((rows, (hs + ht) // 2), f32),
            pltpu.VMEM((2, HALF, vs), f32),
            pltpu.VMEM((2, HALF, vs), f32),
            pltpu.VMEM((2, HALF, 128), f32),
            pltpu.VMEM((2, 8, HALF), f32),
            pltpu.VMEM((2, NZ, 8, HALF), f32),
            pltpu.VMEM((2, 8, HALF), f32),
            pltpu.VMEM((2, NY * NC, 8, HALF), f32),
            pltpu.VMEM((2, HALF, 128), f32),
            pltpu.VMEM((NY, HZ, 2, BLK, 128), f32),
            pltpu.VMEM((2, HALF, hs2), f32),
            pltpu.VMEM((2, HALF, hs2), f32),
            pltpu.VMEM((2, NY, HZ, BLK, hs2), bf16),
            pltpu.VMEM((2, NY, HZ, BLK, sa), bf16),
            pltpu.VMEM((2, HZ, BLK, sa), bf16),
            pltpu.VMEM((2, NZ, BLK, sa), bf16),
            pltpu.VMEM((2, NZ, NY, BLK, hs2 - sa), bf16),
            pltpu.VMEM((2, NY, BLK, hs2 - sa), bf16),
            pltpu.VMEM((2, NY, BLK, hs2 - sa), bf16),
            pltpu.VMEM((NY, HZ, BLK, hs2), f32),
            pltpu.VMEM((8, hs2), f32),
            dma((2,)), dma(()), dma(()),
            dma((2, 2, NZ)), dma((2, 2, NZ)), dma((2, 2, NY)), dma((2, 2, NY)),
            dma((2, 2, NY)), dma((2, 2, NY)), dma((2, 2, NZ)), dma((2, 2, NZ)),
            dma((2, 2)), dma((2, 2)),
            dma((2, NZ)), dma((2, NZ)), dma((2, NY * NC)), dma((2, NY * NC)),
            dma((2,)), dma((2,)),
            dma((2, NY)), dma((2, NY)), dma((2, NZ)), dma((2, NZ)),
            dma((2, NZ)), dma((2, NZ)), dma((2, NY)), dma((2, NY)),
            dma(()), dma(()),
        ],
        compiler_params=pltpu.CompilerParams(
            collective_id=0, has_side_effects=True, vmem_limit_bytes=56 * 1024 * 1024
        ),
        cost_estimate=pl.CostEstimate(
            flops=flops, bytes_accessed=2 * vs * (hs + ht), transcendentals=2 * tokens * vs
        ),
    )(
        student_hidden, teacher_hidden,
        segment_ids.reshape(1, tokens), valid_mask.reshape(1, tokens),
        student_head, teacher_head,
    )
    return kl[:, 2], grad.astype(jnp.bfloat16)


def solution(mesh):
    in_specs = (
        P(("dp", "vocab"), None),
        P(("dp", "vocab"), None),
        P("dp", "vocab"),
        P("dp", "vocab"),
        P("dp"),
        P("dp"),
    )
    out_specs = (P(("dp", "vocab")), P(("dp", "vocab"), None))
    return jax.shard_map(local, mesh=mesh, in_specs=in_specs, out_specs=out_specs, check_vma=False)
```

```python
import functools

import jax
import jax.numpy as jnp
from jax import lax
from jax.experimental import pallas as pl
from jax.experimental.pallas import tpu as pltpu
from jax.sharding import PartitionSpec as P

LOSS_SCALE = 1024.0
NY, NZ, NC = 4, 8, 2
N = 2
HZ = NZ // N
BLK = 16
ROWS = NY * HZ * BLK
TILE = 256
GROUP, PART = 128, 32
SPLIT_S, SPLIT_T, SPLIT_G = 1024, 768, 896
MESH = pl.DeviceIdType.MESH


def kernel(
    hs, ht, vs,
    sh_ref, th_ref, seg_ref, valid_ref, ws_hbm, wt_hbm,
    out_ref,
    ws, wst, wt, x, xf, xg, logit_s, logit_t, exp_s,
    ab, stat_col, stat_own, stat_z, stat_mid, stat_y, fac, wcol,
    gb_rows, ps, pr, r1, ra, r2a, ra2, rb, r2b, rb2, fin, fin_in,
    load_sem, pair_s, pair_r,
    a1_s, a1_r, a2_s, a2_r, b1_s, b1_r, b2_s, b2_r, sib_s, sib_r,
    sz_s, sz_r, sy_s, sy_r, ps_s, ps_r,
    ra1_s, ra1_r, ra2_s, ra2_r, rb1_s, rb1_r, rb2_s, rb2_r, fin_s, fin_r,
):
    v = lax.axis_index("vocab")
    y, z, c = v // (NZ * NC), (v // NC) % NZ, v % NC
    zz, own = z // N, z % N
    hs2, ht2 = hs // 2, ht // 2
    sa, ta = SPLIT_S, SPLIT_T
    ga = SPLIT_G
    gb = hs2 - ga
    widths = ((sa, hs2 - sa), (ta, ht2 - ta))

    def dev(dy, dz, dc):
        return {"vocab": (((y + dy) % NY) * NZ + (z + dz) % NZ) * NC + (c + dc) % NC}

    def rcopy(src, dst, ssem, rsem, device):
        return pltpu.make_async_remote_copy(
            src_ref=src, dst_ref=dst, send_sem=ssem, recv_sem=rsem,
            device_id=device, device_id_type=MESH,
        )

    load_s = pltpu.make_async_copy(ws_hbm, ws, load_sem.at[0])
    load_t = pltpu.make_async_copy(wt_hbm, wt, load_sem.at[1])
    load_s.start()
    load_t.start()

    barrier = pltpu.get_barrier_semaphore()
    partners = [(0, k, 0) for k in range(1, NZ)]
    partners += [(j, 0, d) for j in range(1, NY) for d in range(NC)] + [(0, 0, 1)]
    for p in partners:
        pl.semaphore_signal(barrier, inc=1, device_id=dev(*p), device_id_type=MESH)
    xf[:, :hs2] = sh_ref[:, pl.ds(pl.multiple_of((1 - c) * hs2, 128), hs2)].astype(jnp.float32)
    xf[:, hs2:] = th_ref[:, pl.ds(pl.multiple_of((1 - c) * ht2, 128), ht2)].astype(jnp.float32)
    pl.semaphore_wait(barrier, len(partners))
    pair = rcopy(xf, xg, pair_s, pair_r, dev(0, 0, 1))
    pair.start()

    seg = jnp.broadcast_to(seg_ref[...].astype(jnp.float32), (128, N * ROWS))
    val = jnp.broadcast_to(valid_ref[...].astype(jnp.float32), (128, N * ROWS))
    seg_c, val_c = jnp.transpose(seg)[:, :1], jnp.transpose(val)[:, :1]
    same = jnp.where(seg_c == seg[:1, :], val[:1, :], 0.0)
    count = jnp.sum(same, axis=1, keepdims=True)
    weight = LOSS_SCALE * val_c / jnp.maximum(count, 1.0)
    wcol[...] = jnp.broadcast_to(weight, (N * ROWS, 128)).reshape(NY, HZ, N, BLK, 128)

    pair.wait()

    def put(col, width, full, part):
        mine = full[:, pl.ds(pl.multiple_of(c * width, 128), width)].astype(jnp.float32)
        both = jnp.concatenate(
            [jnp.where(c == 0, mine, part), jnp.where(c == 0, part, mine)], axis=0
        )
        x[own, y, zz, :, pl.ds(pl.multiple_of(col + c * width, 128), width)] = both.astype(
            jnp.bfloat16
        )

    put(0, hs2, sh_ref, xg[:, :hs2])
    put(hs, ht2, th_ref, xg[:, hs2:])

    def cols(u, order, core):
        start = (core * hs2, hs + core * ht2)[u] + (0 if order == 0 else widths[u][0])
        return pl.ds(pl.multiple_of(start, 128), widths[u][order])

    def span(u, core):
        start, width = ((core * hs2, hs2), (hs + core * ht2, ht2))[u]
        return pl.ds(pl.multiple_of(start, 128), width)

    def loop(lo, hi, body):
        def step(i, carry):
            body(i)
            return carry

        lax.fori_loop(lo, hi, step, 0)

    def a1(h, u, k):
        block = x.at[h, y, zz, :, cols(u, 0, c)]
        return rcopy(block, block, a1_s.at[u], a1_r.at[h, u, zz], dev(0, k, 0))

    def a2(h, u, b, j):
        block = x.at[h, y, b, :, cols(u, 0, c)]
        return rcopy(block, block, a2_s.at[u], a2_r.at[h, u], dev(j, 0, 0))

    def b1(h, u, j):
        block = x.at[h, y, zz, :, cols(u, 1, c)]
        return rcopy(block, block, b1_s.at[u], b1_r.at[u], dev(j, 0, 0))

    def b2(h, u, k):
        block = x.at[h, :, zz, :, cols(u, 1, c)]
        return rcopy(block, block, b2_s.at[u], b2_r.at[h, u], dev(0, k, 0))

    def sib(h, u, order):
        block = x.at[h, :, :, :, cols(u, order, c)]
        return rcopy(block, block, sib_s.at[u], sib_r.at[h, u], dev(0, 0, 1))

    flat = x.reshape(N * ROWS, hs + ht)

    def arrived(sem, rows, width):
        some = flat.at[pl.ds(0, rows), pl.ds(0, width)]
        pltpu.make_async_copy(some, some, sem).wait()

    def arrived_f32(sem, like):
        pltpu.make_async_copy(like, like, sem).wait()

    def near_first(k0, count, step, body):
        def some(i):
            k = k0 + step * (i // 2)
            body(jnp.where(i % 2 == 0, k, NZ - k))

        loop(0, count, some)

    def behind(h, body):
        near_first(
            jnp.where(own == h, 2, 1), jnp.where(own == h, HZ - 1, HZ), N, body
        )

    ahead = behind

    def send_first(h, u):
        @pl.when(own == h)
        def _():
            loop(1, NY, lambda j: b1(h, u, j).start())
            near_first(1, NZ - 1, 1, lambda k: a1(h, u, k).start())
            loop(1, NY, lambda j: a2(h, u, zz, j).start())

    def relay(h, u):
        @pl.when(own == h)
        def _():
            arrived(b1_r.at[u], (NY - 1) * BLK, widths[u][1])
            near_first(1, NZ - 1, 1, lambda k: b2(h, u, k).start())

        def onward(k):
            b = ((z - k + NZ) % NZ) // N
            arrived(a1_r.at[h, u, b], BLK, widths[u][0])
            loop(1, NY, lambda j: a2(h, u, b, j).start())

        behind(h, onward)

    def send_sibling(h, u):
        arrived(a2_r.at[h, u], (NY - 1) * HZ * BLK, widths[u][0])
        sib(h, u, 0).start()

        @pl.when(own == h)
        def _():
            arrived(b2_r.at[h, u], (HZ - 1) * NY * BLK, widths[u][1])

        @pl.when(own != h)
        def _():
            arrived(b2_r.at[h, u], HZ * NY * BLK, widths[u][1])

        sib(h, u, 1).start()

    def gathered(u):
        for h in range(N):
            arrived(sib_r.at[h, u], ROWS, (hs2, ht2)[u])

    def student():
        def tile(i):
            at = pl.ds(pl.multiple_of(i * TILE, TILE), TILE)
            rows = x[:, :, :, :, :hs].reshape(N * ROWS, hs)
            logits = jnp.dot(rows, ws[:, at], preferred_element_type=jnp.float32)
            logit_s[:, :, at] = logits.reshape(N, ROWS, TILE)

        loop(0, vs // TILE, tile)

    def teacher():
        def tile(i):
            at = pl.ds(pl.multiple_of(i * TILE, TILE), TILE)
            rows = x[:, :, :, :, hs:].reshape(N * ROWS, ht)
            logits = jnp.dot(rows, wt[:, at], preferred_element_type=jnp.float32)
            logit_t[:, :, at] = logits.reshape(N, ROWS, TILE)

        loop(0, vs // TILE, tile)

    lane = lax.broadcasted_iota(jnp.int32, (1, 128), 1)

    def groups(body):
        def some(i):
            for n in range(GROUP // PART):
                body(pl.ds(pl.multiple_of(i * GROUP + n * PART, PART), PART))

        loop(0, ROWS // GROUP, some)

    def stats_s(h):
        def some(at):
            s = logit_s[h, at, :]
            peak = jnp.max(s, axis=1, keepdims=True)
            e = jnp.exp(s - peak)
            exp_s[h, at, :] = e
            total = jnp.sum(e, axis=1, keepdims=True)
            stat_col[h, at, :] = jnp.where(lane == 0, peak, jnp.where(lane == 1, total, 0.0))

        groups(some)

    def stats_t(h):
        def some(at):
            t = logit_t[h, at, :]
            peak = jnp.max(t, axis=1, keepdims=True)
            total = jnp.sum(jnp.exp(t - peak), axis=1, keepdims=True)
            cross = jnp.sum(exp_s[h, at, :] * (logit_s[h, at, :] - t), axis=1, keepdims=True)
            packed = stat_col[h, at, :]
            mean = cross / packed[:, 1:2]
            for m, value in enumerate((cross, peak, total, mean)):
                packed = jnp.where(lane == m + 2, value, packed)
            stat_col[h, at, :] = packed

        groups(some)

    def sz(h, k):
        return rcopy(stat_own.at[h], stat_z.at[h, k], sz_s, sz_r.at[h], dev(0, k, 0))

    def sy(h, n):
        j, d = n // NC, n % NC
        return rcopy(stat_mid.at[h], stat_y.at[h, n], sy_s, sy_r.at[h], dev(j, 0, d))

    def merge(blocks):
        peak_s = functools.reduce(jnp.maximum, [b[0:1] for b in blocks])
        peak_t = functools.reduce(jnp.maximum, [b[3:4] for b in blocks])
        sum_s = cross = sum_t = 0.0
        for b in blocks:
            scale = jnp.exp(b[0:1] - peak_s)
            sum_s = sum_s + scale * b[1:2]
            cross = cross + scale * b[2:3]
            sum_t = sum_t + jnp.exp(b[3:4] - peak_t) * b[4:5]
        return peak_s, sum_s, cross, peak_t, sum_t

    def stats_z(h):
        stat_own[h] = jnp.transpose(stat_col[h])[:8, :]
        loop(1, NZ, lambda k: sz(h, k).start())

    def stats_y(h):
        arrived_f32(sz_r.at[h], stat_z.at[h, pl.ds(1, NZ - 1)])
        rows = merge([stat_own[h]] + [stat_z[h, k] for k in range(1, NZ)])
        stat_mid[h] = jnp.concatenate(list(rows) + [jnp.zeros((3, ROWS), jnp.float32)], axis=0)
        loop(1, NY * NC, lambda n: sy(h, n).start())

    def factors(h):
        arrived_f32(sy_r.at[h], stat_y.at[h, pl.ds(1, NY * NC - 1)])
        peak_s, sum_s, cross, peak_t, sum_t = merge(
            [stat_mid[h]] + [stat_y[h, n] for n in range(1, NY * NC)]
        )
        lse_s, lse_t = peak_s + jnp.log(sum_s), peak_t + jnp.log(sum_t)
        kl = cross / sum_s - lse_s + lse_t
        offset = lse_s - lse_t + kl
        scale = jnp.exp(stat_own[h][0:1] - lse_s)
        local_mean = stat_own[h][5:6]
        packed = jnp.concatenate(
            [scale, offset - local_mean, kl, jnp.zeros((125, ROWS), jnp.float32)], axis=0
        )
        fac[h] = jnp.transpose(packed)

    def grads(h):
        def some(at):
            e = exp_s[h, at, :]
            ratio = logit_s[h, at, :] - logit_t[h, at, :]
            gb_rows[at, :] = (e * (ratio - stat_col[h, at, 5:6])).astype(jnp.bfloat16)
            gb_rows[pl.ds(ROWS + at.start, PART), :] = e.astype(jnp.bfloat16)

        groups(some)

    part = hs2 // 2

    def transpose(lo, hi):
        def block(i):
            at = pl.ds(pl.multiple_of(i * TILE, TILE), TILE)
            wst[:, at] = jnp.transpose(ws[at, :])

        loop(lo, hi, block)

    def back(h, lo, hi):
        def block(i):
            at = pl.ds(pl.multiple_of(i * 2 * TILE, 2 * TILE), 2 * TILE)
            ab[h, :, at] = jnp.dot(
                gb_rows[...], wst[:, at], preferred_element_type=jnp.float32
            )

        loop(lo, hi, block)

    def mixed(h, core, i):
        w = wcol[:, :, h, :, 0:1].reshape(ROWS, 1)
        at = pl.ds(pl.multiple_of(core * hs2 + i * part, 128), part)
        scale, offset = fac[h, :, 0:1] * w, fac[h, :, 1:2]
        return scale * (ab[h, :ROWS, at] - offset * ab[h, ROWS:, at])

    def swap(h, i):
        return rcopy(ps.at[h, i], pr.at[h, i], ps_s, ps_r.at[h, i], dev(0, 0, 1))

    def ra1(h, j):
        return rcopy(
            r1.at[h, (y + j) % NY, :, :, pl.ds(0, ga)], ra.at[h, j],
            ra1_s, ra1_r.at[h], dev(j, 0, 0),
        )

    def rb1(h, k):
        return rcopy(
            r1.at[h, :, ((z + k) % NZ) // N, :, pl.ds(ga, gb)], rb.at[h, k],
            rb1_s, rb1_r, dev(0, k, 0),
        )

    def rra2(h, k):
        return rcopy(
            r2a.at[h, ((z + k) % NZ) // N], ra2.at[h, k],
            ra2_s, ra2_r, dev(0, k, 0),
        )

    def rrb2(h, j):
        return rcopy(
            r2b.at[h, (y + j) % NY], rb2.at[h, j],
            rb2_s, rb2_r, dev(j, 0, 0),
        )

    def mix(h):
        for i in range(2):
            ps[h, i] = mixed(h, 1 - c, i)
            swap(h, i).start()

    def reduce_first(h):
        for i in range(2):
            total = mixed(h, c, i)
            swap(h, i).wait_recv()
            total = total + pr[h, i]
            r1[h, :, :, :, i * part:(i + 1) * part] = (
                total.astype(jnp.bfloat16).reshape(NY, HZ, BLK, part)
            )
        loop(1, NY, lambda j: ra1(h, j).start())
        ahead(h, lambda k: rb1(h, k).start())

    def reduce_second(h):
        arrived(ra1_r.at[h], (NY - 1) * HZ * BLK, ga)
        total = r1[h, y, :, :, :ga].astype(jnp.float32)
        for j in range(1, NY):
            total = total + ra[h, j].astype(jnp.float32)
        r2a[h] = total.astype(jnp.bfloat16)
        ahead(h, lambda k: rra2(h, k).start())

        @pl.when(own == h)
        def _():
            arrived(rb1_r, (NZ - 1) * NY * BLK, gb)
            total = r1[h, :, zz, :, ga:].astype(jnp.float32)
            for k in range(1, NZ):
                total = total + rb[h, k].astype(jnp.float32)
            r2b[h] = total.astype(jnp.bfloat16)
            loop(1, NY, lambda j: rrb2(h, j).start())

    def final(h):
        @pl.when(own == h)
        def _():
            arrived(ra2_r, (NZ - 1) * BLK, ga)
            arrived(rb2_r, (NY - 1) * BLK, gb)
            left = r2a[h, zz].astype(jnp.float32)
            for k in range(1, NZ):
                left = left + ra2[h, k].astype(jnp.float32)
            right = r2b[h, y].astype(jnp.float32)
            for j in range(1, NY):
                right = right + rb2[h, j].astype(jnp.float32)
            fin[:, :ga] = left
            fin[:, ga:] = right
            give = rcopy(
                fin.at[pl.ds(pl.multiple_of((1 - c) * 8, 8), 8), :], fin_in,
                fin_s, fin_r, dev(0, 0, 1),
            )
            give.start()
            mine = pl.ds(pl.multiple_of(c * hs2, 128), hs2)
            theirs = pl.ds(pl.multiple_of((1 - c) * hs2, 128), hs2)
            out_ref[:, mine] = fin[pl.ds(pl.multiple_of(c * 8, 8), 8), :]
            at = pl.multiple_of((y * HZ + zz) * BLK + c * 8, 8)
            kl = fac[h, pl.ds(at, 8), 2:3]
            row = lax.broadcasted_iota(jnp.int32, (8, 128), 0)
            col = lax.broadcasted_iota(jnp.int32, (8, 128), 1)
            kl = jnp.sum(jnp.where(row == col, kl, 0.0), axis=0, keepdims=True)
            out_ref[:, hs:] = jnp.broadcast_to(kl, (8, 128))
            give.wait()
            out_ref[:, theirs] = fin_in[...]

    def gather_left():
        for u in range(2):
            arrived(a1_s.at[u], (NZ - 1) * BLK, widths[u][0])
            arrived(b1_s.at[u], (NY - 1) * BLK, widths[u][1])
            arrived(b2_s.at[u], (NZ - 1) * NY * BLK, widths[u][1])
            arrived(a2_s.at[u], (NY - 1) * N * HZ * BLK, widths[u][0])
            arrived(sib_s.at[u], N * ROWS, (hs2, ht2)[u])

    def rest_left():
        arrived_f32(sz_s, stat_z.at[:, pl.ds(1, NZ - 1)])
        arrived_f32(sy_s, stat_y.at[:, pl.ds(1, NY * NC - 1)])
        arrived_f32(ps_s, ps)
        arrived(ra1_s, N * (NY - 1) * HZ * BLK, ga)
        arrived(rb1_s, (NZ - 1) * NY * BLK, gb)
        arrived(ra2_s, (NZ - 1) * BLK, ga)
        arrived(rb2_s, (NY - 1) * BLK, gb)

    for u in range(2):
        for h in range(N):
            send_first(h, u)
    load_s.wait()
    transpose(0, hs // TILE)
    for u in range(2):
        for h in range(N):
            relay(h, u)
    load_t.wait()
    for h in range(N):
        send_sibling(h, 0)
    gathered(0)
    student()
    for h in range(N):
        stats_s(h)
    for h in range(N):
        send_sibling(h, 1)
    gathered(1)
    teacher()
    for h in range(N):
        stats_t(h)
        stats_z(h)
    grads(0)
    back(0, 0, 5)
    stats_y(0)
    stats_y(1)
    grads(1)
    back(1, 0, 5)
    factors(0)
    mix(0)
    factors(1)
    mix(1)
    reduce_first(0)
    reduce_first(1)
    reduce_second(0)
    gather_left()
    reduce_second(1)
    for h in range(N):
        final(h)
    rest_left()


def split(result_ref, kl_ref, grad_ref):
    rows, hs = grad_ref.shape
    kl_ref[...] = result_ref[:1, hs:hs + rows]
    grad_ref[...] = result_ref[:, :hs].astype(jnp.bfloat16)


def local(student_hidden, teacher_hidden, student_head, teacher_head, segment_ids, valid_mask):
    rows, hs = student_hidden.shape
    ht = teacher_hidden.shape[1]
    vs = student_head.shape[1]
    tokens = segment_ids.shape[0]
    hs2 = hs // 2
    ga, gb = SPLIT_G, hs2 - SPLIT_G
    f32, bf16 = jnp.float32, jnp.bfloat16
    dma = pltpu.SemaphoreType.DMA
    vmem = pl.BlockSpec(memory_space=pltpu.VMEM)
    hbm = pl.BlockSpec(memory_space=pl.ANY)
    flops = 2 * tokens * vs * (2 * hs + ht)
    result = pl.pallas_call(
        functools.partial(kernel, hs, ht, vs),
        out_shape=jax.ShapeDtypeStruct((rows, hs + 128), f32),
        in_specs=[vmem, vmem, vmem, vmem, hbm, hbm],
        out_specs=vmem,
        scratch_shapes=[
            pltpu.VMEM((hs, vs), bf16),
            pltpu.VMEM((vs, hs), bf16),
            pltpu.VMEM((ht, vs), bf16),
            pltpu.VMEM((N, NY, HZ, BLK, hs + ht), bf16),
            pltpu.VMEM((rows, (hs + ht) // 2), f32),
            pltpu.VMEM((rows, (hs + ht) // 2), f32),
            pltpu.VMEM((N, ROWS, vs), f32),
            pltpu.VMEM((N, ROWS, vs), f32),
            pltpu.VMEM((N, ROWS, vs), f32),
            pltpu.VMEM((N, 2 * ROWS, hs), f32),
            pltpu.VMEM((N, ROWS, 128), f32),
            pltpu.VMEM((N, 8, ROWS), f32),
            pltpu.VMEM((N, NZ, 8, ROWS), f32),
            pltpu.VMEM((N, 8, ROWS), f32),
            pltpu.VMEM((N, NY * NC, 8, ROWS), f32),
            pltpu.VMEM((N, ROWS, 128), f32),
            pltpu.VMEM((NY, HZ, N, BLK, 128), f32),
            pltpu.VMEM((2 * ROWS, vs), bf16),
            pltpu.VMEM((N, 2, ROWS, hs2 // 2), f32),
            pltpu.VMEM((N, 2, ROWS, hs2 // 2), f32),
            pltpu.VMEM((N, NY, HZ, BLK, hs2), bf16),
            pltpu.VMEM((N, NY, HZ, BLK, ga), bf16),
            pltpu.VMEM((N, HZ, BLK, ga), bf16),
            pltpu.VMEM((N, NZ, BLK, ga), bf16),
            pltpu.VMEM((N, NZ, NY, BLK, gb), bf16),
            pltpu.VMEM((N, NY, BLK, gb), bf16),
            pltpu.VMEM((N, NY, BLK, gb), bf16),
            pltpu.VMEM((BLK, hs2), f32),
            pltpu.VMEM((8, hs2), f32),
            dma((2,)), dma(()), dma(()),
            dma((2,)), dma((N, 2, HZ)), dma((2,)), dma((N, 2)),
            dma((2,)), dma((2,)), dma((2,)), dma((N, 2)),
            dma((2,)), dma((N, 2)),
            dma(()), dma((N,)), dma(()), dma((N,)), dma(()), dma((N, 2)),
            dma(()), dma((N,)), dma(()), dma(()),
            dma(()), dma(()), dma(()), dma(()),
            dma(()), dma(()),
        ],
        compiler_params=pltpu.CompilerParams(
            collective_id=0, has_side_effects=True, vmem_limit_bytes=56 * 1024 * 1024
        ),
        cost_estimate=pl.CostEstimate(
            flops=flops, bytes_accessed=2 * vs * (hs + ht), transcendentals=2 * tokens * vs
        ),
    )(
        student_hidden, teacher_hidden,
        segment_ids.reshape(1, tokens), valid_mask.reshape(1, tokens),
        student_head, teacher_head,
    )
    kl, grad = pl.pallas_call(
        split,
        out_shape=(jax.ShapeDtypeStruct((1, rows), f32), jax.ShapeDtypeStruct((rows, hs), bf16)),
        in_specs=[vmem],
        out_specs=(vmem, vmem),
    )(result)
    return kl.reshape(rows), grad


def solution(mesh):
    in_specs = (
        P(("dp", "vocab"), None),
        P(("dp", "vocab"), None),
        P("dp", "vocab"),
        P("dp", "vocab"),
        P("dp"),
        P("dp"),
    )
    out_specs = (P(("dp", "vocab")), P(("dp", "vocab"), None))
    return jax.shard_map(local, mesh=mesh, in_specs=in_specs, out_specs=out_specs, check_vma=False)
```

```python
import functools

import jax
import jax.numpy as jnp
from jax import lax
from jax.experimental import pallas as pl
from jax.experimental.pallas import tpu as pltpu
from jax.sharding import PartitionSpec as P

LOSS_SCALE = 1024.0
NY, NZ, NC = 4, 8, 2
N = 2
HZ = NZ // N
BLK = 16
ROWS = NY * HZ * BLK
TILE = 256
GROUP, PART = 128, 32
SPLIT_S, SPLIT_T, SPLIT_G = 1024, 768, 896
MESH = pl.DeviceIdType.MESH


def kernel(
    hs, ht, vs,
    sh_ref, th_ref, seg_ref, valid_ref, ws_hbm, wt_hbm,
    out_ref,
    ws, w_in, wst, wt, x, xf, xg, logit_s, logit_t, exp_s,
    sum_e, sum_a, stat_col, stat_own, stat_sib, stat_z, stat_mid, stat_y, fac, wcol,
    e_rows, e_in, a_rows, a_in, r1, ra, r2a, ra2, rb, r2b, rb2, fin, fin_in,
    load_sem, pair_s, pair_r,
    a1_s, a1_r, a2_s, a2_r, a2f_r, a3_r, b1_s, b1_r, b2_s, b2_r, b2f_r, sib_s, sib_r,
    sz_s, sz_r, sy_s, sy_r, w_s, w_r, ss_s, ss_r, ge_s, ge_r, ga_s, ga_r,
    ra1_s, ra1_r, ra2_s, ra2_r, rb1_s, rb1_r, rb2_s, rb2_r, fin_s, fin_r,
):
    v = lax.axis_index("vocab")
    y, z, c = v // (NZ * NC), (v // NC) % NZ, v % NC
    zz, own = z // N, z % N
    hs2, ht2 = hs // 2, ht // 2
    sa, ta = SPLIT_S, SPLIT_T
    ga = SPLIT_G
    gb = hs2 - ga
    widths = ((sa, hs2 - sa), (ta, ht2 - ta))

    def dev(dy, dz, dc):
        return {"vocab": (((y + dy) % NY) * NZ + (z + dz) % NZ) * NC + (c + dc) % NC}

    def rcopy(src, dst, ssem, rsem, device):
        return pltpu.make_async_remote_copy(
            src_ref=src, dst_ref=dst, send_sem=ssem, recv_sem=rsem,
            device_id=device, device_id_type=MESH,
        )

    load_s = pltpu.make_async_copy(ws_hbm, ws, load_sem.at[0])
    load_t = pltpu.make_async_copy(wt_hbm, wt, load_sem.at[1])
    load_s.start()
    load_t.start()

    barrier = pltpu.get_barrier_semaphore()
    partners = [(0, k, 0) for k in range(1, NZ)]
    partners += [(j, 0, d) for j in range(1, NY) for d in range(NC)] + [(0, 0, 1)]
    for p in partners:
        pl.semaphore_signal(barrier, inc=1, device_id=dev(*p), device_id_type=MESH)
    xf[:, :hs2] = sh_ref[:, pl.ds(pl.multiple_of((1 - c) * hs2, 128), hs2)].astype(jnp.float32)
    xf[:, hs2:] = th_ref[:, pl.ds(pl.multiple_of((1 - c) * ht2, 128), ht2)].astype(jnp.float32)
    pl.semaphore_wait(barrier, len(partners))
    pair = rcopy(xf, xg, pair_s, pair_r, dev(0, 0, 1))
    pair.start()

    seg = jnp.broadcast_to(seg_ref[...].astype(jnp.float32), (128, N * ROWS))
    val = jnp.broadcast_to(valid_ref[...].astype(jnp.float32), (128, N * ROWS))
    seg_c, val_c = jnp.transpose(seg)[:, :1], jnp.transpose(val)[:, :1]
    same = jnp.where(seg_c == seg[:1, :], val[:1, :], 0.0)
    count = jnp.sum(same, axis=1, keepdims=True)
    weight = LOSS_SCALE * val_c / jnp.maximum(count, 1.0)
    wcol[...] = jnp.broadcast_to(weight, (N * ROWS, 128)).reshape(NY, HZ, N, BLK, 128)

    pair.wait()

    def put(col, width, full, part):
        mine = full[:, pl.ds(pl.multiple_of(c * width, 128), width)].astype(jnp.float32)
        both = jnp.concatenate(
            [jnp.where(c == 0, mine, part), jnp.where(c == 0, part, mine)], axis=0
        )
        x[own, y, zz, :, pl.ds(pl.multiple_of(col + c * width, 128), width)] = both.astype(
            jnp.bfloat16
        )

    put(0, hs2, sh_ref, xg[:, :hs2])
    put(hs, ht2, th_ref, xg[:, hs2:])

    def cols(u, order, core):
        start = (core * hs2, hs + core * ht2)[u] + (0 if order == 0 else widths[u][0])
        return pl.ds(pl.multiple_of(start, 128), widths[u][order])

    def span(u, core):
        start, width = ((core * hs2, hs2), (hs + core * ht2, ht2))[u]
        return pl.ds(pl.multiple_of(start, 128), width)

    def loop(lo, hi, body):
        def step(i, carry):
            body(i)
            return carry

        lax.fori_loop(lo, hi, step, 0)

    def a1(u, k, ahead):
        source = (z - k + NZ) % NZ
        h, b = source % N, source // N
        block = x.at[h, y, b, :, cols(u, 0, c)]
        return rcopy(block, block, a1_s.at[u], a1_r.at[h, u, b], dev(0, ahead, 0))

    onward, back_y = jnp.where(c == 0, 1, NY - 1), jnp.where(c == 0, NY - 1, 1)

    def a2_on(h, u, b, late):
        block = x.at[h, y, b, :, cols(u, 0, c)]
        return rcopy(block, block, a2_s.at[u], a2f_r.at[u, late], dev(onward, 0, 0))

    def a2_back(h, u, b):
        block = x.at[h, y, b, :, cols(u, 0, c)]
        return rcopy(block, block, a2_s.at[u], a2_r.at[h, u], dev(back_y, 0, 0))

    def a3(u, k):
        source = (z - k + NZ) % NZ
        h, b = source % N, source // N
        block = x.at[h, (y + back_y) % NY, b, :, cols(u, 0, c)]
        return rcopy(block, block, a2_s.at[u], a3_r.at[h, u], dev(onward, 0, 0))

    def b1(h, u, j):
        block = x.at[h, y, zz, :, cols(u, 1, c)]
        return rcopy(block, block, b1_s.at[u], b1_r.at[u], dev(j, 0, 0))

    def b2(u, k, ahead, sem):
        source = (z - k + NZ) % NZ
        block = x.at[source % N, :, source // N, :, cols(u, 1, c)]
        return rcopy(block, block, b2_s.at[u], sem, dev(0, ahead, 0))

    def sib_a(h, u, dy):
        block = x.at[h, (y + dy) % NY, :, :, cols(u, 0, c)]
        return rcopy(block, block, sib_s.at[u], sib_r.at[h, u], dev(0, 0, 1))

    def sib_b(h, u):
        block = x.at[h, :, :, :, cols(u, 1, c)]
        return rcopy(block, block, sib_s.at[u], sib_r.at[h, u], dev(0, 0, 1))

    flat = x.reshape(N * ROWS, hs + ht)

    def arrived(sem, rows, width):
        some = flat.at[pl.ds(0, rows), pl.ds(0, width)]
        pltpu.make_async_copy(some, some, sem).wait()

    def arrived_f32(sem, like):
        pltpu.make_async_copy(like, like, sem).wait()

    def near_first(k0, count, step, body):
        def some(i):
            k = k0 + step * (i // 2)
            body(jnp.where(i % 2 == 0, k, NZ - k))

        loop(0, count, some)

    def behind(h, body):
        near_first(
            jnp.where(own == h, 2, 1), jnp.where(own == h, HZ - 1, HZ), N, body
        )

    ahead = behind

    def send_first(u):
        loop(1, NY, lambda j: b1(own, u, j).start())
        a1(u, 0, 1).start()
        a1(u, 0, NZ - 1).start()
        a2_on(own, u, zz, 0).start()
        a2_back(own, u, zz).start()
        a1(u, 0, 2).start()
        a1(u, 0, NZ - 2).start()

    direct, relayed = (1, NZ - 1, 2, NZ - 2), (3, NZ - 3, 4)

    def relay(u, late):
        for k in (direct, relayed)[late]:
            source = (z - k + NZ) % NZ
            h, b = source % N, source // N
            arrived(a1_r.at[h, u, b], BLK, widths[u][0])
            if k == 2:
                a1(u, k, 1).start()

                @pl.when(c == 0)
                def _():
                    a1(u, k, 2).start()

            if k == NZ - 2:
                a1(u, k, NZ - 1).start()

                @pl.when(c == 1)
                def _():
                    a1(u, k, NZ - 2).start()

            a2_on(h, u, b, late).start()
            a2_back(h, u, b).start()

    def relay_b(u):
        arrived(b1_r.at[u], (NY - 1) * BLK, widths[u][1])
        b2(u, 0, 2, b2f_r.at[u, 0]).start()
        b2(u, 0, NZ - 2, b2f_r.at[u, 1]).start()
        b2(u, 0, 1, b2_r.at[u]).start()
        b2(u, 0, NZ - 1, b2_r.at[u]).start()

    def relay_b2(u):
        arrived(b2f_r.at[u, 0], NY * BLK, widths[u][1])
        b2(u, 2, 1, b2_r.at[u]).start()

        @pl.when(c == 0)
        def _():
            b2(u, 2, 2, b2_r.at[u]).start()

        arrived(b2f_r.at[u, 1], NY * BLK, widths[u][1])
        b2(u, NZ - 2, NZ - 1, b2_r.at[u]).start()

        @pl.when(c == 1)
        def _():
            b2(u, NZ - 2, NZ - 2, b2_r.at[u]).start()

    def relay_y(u, late):
        ks = ((0,) + direct, relayed)[late]
        arrived(a2f_r.at[u, late], len(ks) * BLK, widths[u][0])
        for k in ks:
            a3(u, k).start()
        if late:
            for h in range(N):
                sib_a(h, u, back_y).start()

    def send_sibling_own(u):
        for h in range(N):
            sib_a(h, u, 0).start()

    def send_sibling_b(u):
        arrived(b2_r.at[u], 5 * NY * BLK, widths[u][1])
        for h in range(N):
            sib_b(h, u).start()

    def send_sibling_a(h, u):
        arrived(a2_r.at[h, u], HZ * BLK, widths[u][0])
        sib_a(h, u, onward).start()

    def send_sibling_last(h, u):
        arrived(a3_r.at[h, u], HZ * BLK, widths[u][0])
        sib_a(h, u, 2).start()

    def gathered(u):
        for h in range(N):
            arrived(sib_r.at[h, u], ROWS, (hs2, ht2)[u])

    def student(core, add):
        def tile(i):
            at = pl.ds(pl.multiple_of(i * (vs // 2), 128), vs // 2)
            rows = x[:, :, :, :, span(0, core)].reshape(N * ROWS, hs2)
            logits = jnp.dot(rows, ws[span(0, core), at], preferred_element_type=jnp.float32)
            logits = logits.reshape(N, ROWS, vs // 2)
            logit_s[:, :, at] = logit_s[:, :, at] + logits if add else logits

        loop(0, 2, tile)

    wt_span = lambda core: pl.ds(pl.multiple_of(core * ht2, 128), ht2)

    def teacher_own():
        def tile(i):
            at = pl.ds(pl.multiple_of(i * (vs // 2), 128), vs // 2)
            rows = x[:, :, :, :, span(1, c)].reshape(N * ROWS, ht2)
            logits = jnp.dot(rows, wt[wt_span(c), at], preferred_element_type=jnp.float32)
            logit_t[:, :, at] = logits.reshape(N, ROWS, vs // 2)

        loop(0, 2, tile)

    def teacher(h):
        def tile(i):
            at = pl.ds(pl.multiple_of(i * (vs // 2), 128), vs // 2)
            rows = x[h, :, :, :, span(1, 1 - c)].reshape(ROWS, ht2)
            logits = jnp.dot(rows, wt[wt_span(1 - c), at], preferred_element_type=jnp.float32)
            logit_t[h, :, at] = logit_t[h, :, at] + logits

        loop(0, 2, tile)

    lane = lax.broadcasted_iota(jnp.int32, (1, 128), 1)

    def groups(body):
        def some(i):
            for n in range(GROUP // PART):
                body(pl.ds(pl.multiple_of(i * GROUP + n * PART, PART), PART))

        loop(0, ROWS // GROUP, some)

    def stats_s(h):
        def some(at):
            s = logit_s[h, at, :]
            peak = jnp.max(s, axis=1, keepdims=True)
            e = jnp.exp(s - peak)
            exp_s[h, at, :] = e
            total = jnp.sum(e, axis=1, keepdims=True)
            stat_col[h, at, :] = jnp.where(lane == 0, peak, jnp.where(lane == 1, total, 0.0))

        groups(some)

    def stats_t(h):
        def some(at):
            t = logit_t[h, at, :]
            peak = jnp.max(t, axis=1, keepdims=True)
            total = jnp.sum(jnp.exp(t - peak), axis=1, keepdims=True)
            cross = jnp.sum(exp_s[h, at, :] * (logit_s[h, at, :] - t), axis=1, keepdims=True)
            packed = stat_col[h, at, :]
            mean = cross / packed[:, 1:2]
            for m, value in enumerate((cross, peak, total, mean)):
                packed = jnp.where(lane == m + 2, value, packed)
            stat_col[h, at, :] = packed

        groups(some)

    def sz(h, k):
        return rcopy(stat_own.at[h], stat_z.at[h, k], sz_s, sz_r.at[h], dev(0, k, 0))

    def sy(h, n):
        j, d = n // NC, n % NC
        return rcopy(stat_mid.at[h], stat_y.at[h, n], sy_s, sy_r.at[h], dev(j, 0, d))

    def merge(blocks):
        peak_s = functools.reduce(jnp.maximum, [b[0:1] for b in blocks])
        peak_t = functools.reduce(jnp.maximum, [b[3:4] for b in blocks])
        sum_s = cross = sum_t = 0.0
        for b in blocks:
            scale = jnp.exp(b[0:1] - peak_s)
            sum_s = sum_s + scale * b[1:2]
            cross = cross + scale * b[2:3]
            sum_t = sum_t + jnp.exp(b[3:4] - peak_t) * b[4:5]
        return peak_s, sum_s, cross, peak_t, sum_t

    def to_sibling(src, dst, ssem, rsem):
        return rcopy(src, dst, ssem, rsem, dev(0, 0, 1))

    def stats_sib(h):
        return to_sibling(stat_own.at[h], stat_sib.at[h], ss_s, ss_r.at[h])

    def stats_z(h):
        stat_own[h] = jnp.transpose(stat_col[h])[:8, :]
        stats_sib(h).start()
        loop(1, NZ, lambda k: sz(h, k).start())

    def stats_y(h):
        arrived_f32(sz_r.at[h], stat_z.at[h, pl.ds(1, NZ - 1)])
        rows = merge([stat_own[h]] + [stat_z[h, k] for k in range(1, NZ)])
        stat_mid[h] = jnp.concatenate(list(rows) + [jnp.zeros((3, ROWS), jnp.float32)], axis=0)
        loop(1, NY * NC, lambda n: sy(h, n).start())

    def factors(h):
        arrived_f32(sy_r.at[h], stat_y.at[h, pl.ds(1, NY * NC - 1)])
        peak_s, sum_s, cross, peak_t, sum_t = merge(
            [stat_mid[h]] + [stat_y[h, n] for n in range(1, NY * NC)]
        )
        lse_s, lse_t = peak_s + jnp.log(sum_s), peak_t + jnp.log(sum_t)
        kl = cross / sum_s - lse_s + lse_t
        offset = lse_s - lse_t + kl
        stats_sib(h).wait_recv()
        both = []
        for stat in (stat_own[h], stat_sib[h]):
            both += [jnp.exp(stat[0:1] - lse_s), offset - stat[5:6]]
        packed = jnp.concatenate(both + [kl, jnp.zeros((123, ROWS), jnp.float32)], axis=0)
        fac[h] = jnp.transpose(packed)

    def e_sib():
        return to_sibling(e_rows, e_in, ge_s, ge_r)

    def a_sib(h):
        return to_sibling(a_rows.at[h], a_in.at[h], ga_s, ga_r.at[h])

    def head_sib():
        return to_sibling(ws.at[span(0, 1 - c)], w_in, w_s, w_r)

    def grads_e():
        for h in range(N):
            def some(at):
                e_rows[h, at, :] = exp_s[h, at, :].astype(jnp.bfloat16)

            groups(some)
        e_sib().start()

    def grads_a(h):
        def some(at):
            ratio = logit_s[h, at, :] - logit_t[h, at, :]
            a = exp_s[h, at, :] * (ratio - stat_col[h, at, 5:6])
            a_rows[h, at, :] = a.astype(jnp.bfloat16)

        groups(some)
        a_sib(h).start()

    part = hs2 // 2

    def transpose(n, src, start):
        def block(i):
            at = pl.ds(pl.multiple_of(i * TILE, TILE), TILE)
            rows = pl.ds(pl.multiple_of(start + i * TILE, TILE), TILE)
            wst[n, :, at] = jnp.transpose(src[rows, :])

        loop(0, hs2 // TILE, block)

    def back_e(n, lo, hi):
        def block(i):
            at = pl.ds(pl.multiple_of(i * part, 128), part)
            rows = (e_rows, e_in)[n][...].reshape(N * ROWS, vs)
            sums = jnp.dot(rows, wst[n, :, at], preferred_element_type=jnp.float32)
            sum_e[n, :, :, at] = sums.reshape(N, ROWS, part)

        loop(lo, hi, block)

    def back_a(h, n):
        def block(i):
            at = pl.ds(pl.multiple_of(i * part, 128), part)
            rows = (a_rows, a_in)[n][h]
            sum_a[n, h, :, at] = jnp.dot(rows, wst[n, :, at], preferred_element_type=jnp.float32)

        loop(0, 2, block)

    def ra1(h, j):
        return rcopy(
            r1.at[h, (y + j) % NY, :, :, pl.ds(0, ga)], ra.at[h, j],
            ra1_s, ra1_r.at[h], dev(j, 0, 0),
        )

    def rb1(h, k):
        return rcopy(
            r1.at[h, :, ((z + k) % NZ) // N, :, pl.ds(ga, gb)], rb.at[h, k],
            rb1_s, rb1_r, dev(0, k, 0),
        )

    def rra2(h, k):
        return rcopy(
            r2a.at[h, ((z + k) % NZ) // N], ra2.at[h, k],
            ra2_s, ra2_r, dev(0, k, 0),
        )

    def rrb2(h, j):
        return rcopy(
            r2b.at[h, (y + j) % NY], rb2.at[h, j],
            rb2_s, rb2_r, dev(j, 0, 0),
        )

    def reduce_first(h):
        w = wcol[:, :, h, :, 0:1].reshape(ROWS, 1)
        f = [fac[h, :, n:n + 1] for n in range(4)]
        for i in range(2):
            at = slice(i * part, (i + 1) * part)
            total = 0.0
            for n in range(2):
                some = sum_a[n, h, :, at] - f[2 * n + 1] * sum_e[n, h, :, at]
                total = total + (f[2 * n] * w) * some
            r1[h, :, :, :, at] = total.astype(jnp.bfloat16).reshape(NY, HZ, BLK, part)
        loop(1, NY, lambda j: ra1(h, j).start())
        ahead(h, lambda k: rb1(h, k).start())

    def reduce_second(h):
        arrived(ra1_r.at[h], (NY - 1) * HZ * BLK, ga)
        total = r1[h, y, :, :, :ga].astype(jnp.float32)
        for j in range(1, NY):
            total = total + ra[h, j].astype(jnp.float32)
        r2a[h] = total.astype(jnp.bfloat16)
        ahead(h, lambda k: rra2(h, k).start())

        @pl.when(own == h)
        def _():
            arrived(rb1_r, (NZ - 1) * NY * BLK, gb)
            total = r1[h, :, zz, :, ga:].astype(jnp.float32)
            for k in range(1, NZ):
                total = total + rb[h, k].astype(jnp.float32)
            r2b[h] = total.astype(jnp.bfloat16)
            loop(1, NY, lambda j: rrb2(h, j).start())

    def final(h):
        @pl.when(own == h)
        def _():
            arrived(ra2_r, (NZ - 1) * BLK, ga)
            arrived(rb2_r, (NY - 1) * BLK, gb)
            left = r2a[h, zz].astype(jnp.float32)
            for k in range(1, NZ):
                left = left + ra2[h, k].astype(jnp.float32)
            right = r2b[h, y].astype(jnp.float32)
            for j in range(1, NY):
                right = right + rb2[h, j].astype(jnp.float32)
            fin[:, :ga] = left
            fin[:, ga:] = right
            give = rcopy(
                fin.at[pl.ds(pl.multiple_of((1 - c) * 8, 8), 8), :], fin_in,
                fin_s, fin_r, dev(0, 0, 1),
            )
            give.start()
            mine = pl.ds(pl.multiple_of(c * hs2, 128), hs2)
            theirs = pl.ds(pl.multiple_of((1 - c) * hs2, 128), hs2)
            out_ref[:, mine] = fin[pl.ds(pl.multiple_of(c * 8, 8), 8), :]
            at = pl.multiple_of((y * HZ + zz) * BLK + c * 8, 8)
            kl = fac[h, pl.ds(at, 8), 4:5]
            row = lax.broadcasted_iota(jnp.int32, (8, 128), 0)
            col = lax.broadcasted_iota(jnp.int32, (8, 128), 1)
            kl = jnp.sum(jnp.where(row == col, kl, 0.0), axis=0, keepdims=True)
            out_ref[:, hs:] = jnp.broadcast_to(kl, (8, 128))
            give.wait()
            out_ref[:, theirs] = fin_in[...]

    def gather_left():
        for u in range(2):
            arrived(a1_s.at[u], (NZ - 1) * BLK, widths[u][0])
            arrived(b1_s.at[u], (NY - 1) * BLK, widths[u][1])
            arrived(b2_s.at[u], (NZ - 1) * NY * BLK, widths[u][1])
            arrived(a2_s.at[u], (NY - 1) * N * HZ * BLK, widths[u][0])
            arrived(sib_s.at[u], N * ROWS, (hs2, ht2)[u])

    def rest_left():
        arrived_f32(sz_s, stat_z.at[:, pl.ds(1, NZ - 1)])
        arrived_f32(sy_s, stat_y.at[:, pl.ds(1, NY * NC - 1)])
        head_sib().wait_send()
        arrived_f32(ss_s, stat_sib)
        arrived_f32(ge_s, e_rows)
        arrived_f32(ga_s, a_rows)
        arrived(ra1_s, N * (NY - 1) * HZ * BLK, ga)
        arrived(rb1_s, (NZ - 1) * NY * BLK, gb)
        arrived(ra2_s, (NZ - 1) * BLK, ga)
        arrived(rb2_s, (NY - 1) * BLK, gb)

    for u in range(2):
        send_first(u)
    load_s.wait()
    head_sib().start()
    transpose(0, ws, c * hs2)
    relay_b(0)
    relay(0, 0)
    relay_b(1)
    relay(1, 0)
    relay(0, 1)
    relay_b2(0)
    send_sibling_own(0)
    relay_y(0, 0)
    relay(1, 1)
    relay_y(0, 1)
    relay_b2(1)
    send_sibling_own(1)
    relay_y(1, 0)
    head_sib().wait_recv()
    transpose(1, w_in, 0)
    relay_y(1, 1)
    load_t.wait()
    for h in range(N):
        send_sibling_a(h, 0)
    send_sibling_b(0)
    for h in range(N):
        send_sibling_last(h, 0)
    student(c, False)
    gathered(0)
    student(1 - c, True)
    for h in range(N):
        send_sibling_a(h, 1)
    send_sibling_b(1)
    for h in range(N):
        stats_s(h)
    for h in range(N):
        send_sibling_last(h, 1)
    teacher_own()
    grads_e()
    gathered(1)
    for h in range(N):
        teacher(h)
        stats_t(h)
        stats_z(h)
    for h in range(N):
        grads_a(h)
    back_e(0, 0, 2)
    stats_y(0)
    back_a(0, 0)
    stats_y(1)
    e_sib().wait_recv()
    back_e(1, 0, 2)
    a_sib(0).wait_recv()
    back_a(0, 1)
    factors(0)
    reduce_first(0)
    back_a(1, 0)
    a_sib(1).wait_recv()
    back_a(1, 1)
    factors(1)
    reduce_first(1)
    reduce_second(0)
    gather_left()
    reduce_second(1)
    for h in range(N):
        final(h)
    rest_left()


def split(result_ref, kl_ref, grad_ref):
    rows, hs = grad_ref.shape
    kl_ref[...] = result_ref[:1, hs:hs + rows]
    grad_ref[...] = result_ref[:, :hs].astype(jnp.bfloat16)


def local(student_hidden, teacher_hidden, student_head, teacher_head, segment_ids, valid_mask):
    rows, hs = student_hidden.shape
    ht = teacher_hidden.shape[1]
    vs = student_head.shape[1]
    tokens = segment_ids.shape[0]
    hs2 = hs // 2
    ga, gb = SPLIT_G, hs2 - SPLIT_G
    f32, bf16 = jnp.float32, jnp.bfloat16
    dma = pltpu.SemaphoreType.DMA
    vmem = pl.BlockSpec(memory_space=pltpu.VMEM)
    hbm = pl.BlockSpec(memory_space=pl.ANY)
    flops = 2 * tokens * vs * (2 * hs + ht)
    result = pl.pallas_call(
        functools.partial(kernel, hs, ht, vs),
        out_shape=jax.ShapeDtypeStruct((rows, hs + 128), f32),
        in_specs=[vmem, vmem, vmem, vmem, hbm, hbm],
        out_specs=vmem,
        scratch_shapes=[
            pltpu.VMEM((hs, vs), bf16),
            pltpu.VMEM((hs2, vs), bf16),
            pltpu.VMEM((2, vs, hs2), bf16),
            pltpu.VMEM((ht, vs), bf16),
            pltpu.VMEM((N, NY, HZ, BLK, hs + ht), bf16),
            pltpu.VMEM((rows, (hs + ht) // 2), f32),
            pltpu.VMEM((rows, (hs + ht) // 2), f32),
            pltpu.VMEM((N, ROWS, vs), f32),
            pltpu.VMEM((N, ROWS, vs), f32),
            pltpu.VMEM((N, ROWS, vs), f32),
            pltpu.VMEM((2, N, ROWS, hs2), f32),
            pltpu.VMEM((2, N, ROWS, hs2), f32),
            pltpu.VMEM((N, ROWS, 128), f32),
            pltpu.VMEM((N, 8, ROWS), f32),
            pltpu.VMEM((N, 8, ROWS), f32),
            pltpu.VMEM((N, NZ, 8, ROWS), f32),
            pltpu.VMEM((N, 8, ROWS), f32),
            pltpu.VMEM((N, NY * NC, 8, ROWS), f32),
            pltpu.VMEM((N, ROWS, 128), f32),
            pltpu.VMEM((NY, HZ, N, BLK, 128), f32),
            pltpu.VMEM((N, ROWS, vs), bf16),
            pltpu.VMEM((N, ROWS, vs), bf16),
            pltpu.VMEM((N, ROWS, vs), bf16),
            pltpu.VMEM((N, ROWS, vs), bf16),
            pltpu.VMEM((N, NY, HZ, BLK, hs2), bf16),
            pltpu.VMEM((N, NY, HZ, BLK, ga), bf16),
            pltpu.VMEM((N, HZ, BLK, ga), bf16),
            pltpu.VMEM((N, NZ, BLK, ga), bf16),
            pltpu.VMEM((N, NZ, NY, BLK, gb), bf16),
            pltpu.VMEM((N, NY, BLK, gb), bf16),
            pltpu.VMEM((N, NY, BLK, gb), bf16),
            pltpu.VMEM((BLK, hs2), f32),
            pltpu.VMEM((8, hs2), f32),
            dma((2,)), dma(()), dma(()),
            dma((2,)), dma((N, 2, HZ)), dma((2,)), dma((N, 2)), dma((N, 2)), dma((N, 2)),
            dma((2,)), dma((2,)), dma((2,)), dma((2,)), dma((2, 2)),
            dma((2,)), dma((N, 2)),
            dma(()), dma((N,)), dma(()), dma((N,)), dma(()), dma(()), dma(()), dma((N,)),
            dma(()), dma(()), dma(()), dma((N,)),
            dma(()), dma((N,)), dma(()), dma(()),
            dma(()), dma(()), dma(()), dma(()),
            dma(()), dma(()),
        ],
        compiler_params=pltpu.CompilerParams(
            collective_id=0, has_side_effects=True, vmem_limit_bytes=60 * 1024 * 1024
        ),
        cost_estimate=pl.CostEstimate(
            flops=flops, bytes_accessed=2 * vs * (hs + ht), transcendentals=2 * tokens * vs
        ),
    )(
        student_hidden, teacher_hidden,
        segment_ids.reshape(1, tokens), valid_mask.reshape(1, tokens),
        student_head, teacher_head,
    )
    kl, grad = pl.pallas_call(
        split,
        out_shape=(jax.ShapeDtypeStruct((1, rows), f32), jax.ShapeDtypeStruct((rows, hs), bf16)),
        in_specs=[vmem],
        out_specs=(vmem, vmem),
    )(result)
    return kl.reshape(rows), grad


def solution(mesh):
    in_specs = (
        P(("dp", "vocab"), None),
        P(("dp", "vocab"), None),
        P("dp", "vocab"),
        P("dp", "vocab"),
        P("dp"),
        P("dp"),
    )
    out_specs = (P(("dp", "vocab")), P(("dp", "vocab"), None))
    return jax.shard_map(local, mesh=mesh, in_specs=in_specs, out_specs=out_specs, check_vma=False)
```

```python
import functools

import jax
import jax.numpy as jnp
from jax import lax
from jax.experimental import pallas as pl
from jax.experimental.pallas import tpu as pltpu
from jax.sharding import PartitionSpec as P

LOSS_SCALE = 1024.0
NY, NZ, NC = 4, 8, 2
N = 2
HZ = NZ // N
BLK = 16
ROWS = NY * HZ * BLK
TILE = 256
GROUP, PART = 128, 32
SPLIT_S, SPLIT_T, SPLIT_G = 1024, 640, 896
MESH = pl.DeviceIdType.MESH


def wide_half(width):
    return (width + 255) // 256 * 128


def kernel(
    hs, ht, vs,
    sh_ref, th_ref, seg_ref, valid_ref, ws_hbm, wt_hbm,
    out_ref,
    ws, w_in, wst, wt, x, xf, xg, logit_s, logit_t, exp_s,
    sum_e, sum_a, stat_col, stat_own, stat_sib, stat_z, stat_mid, stat_y, fac, wcol,
    e_rows, e_in, a_rows, a_in, r1, ra, r2a, ra2, rb, r2b, rb2,
    load_sem, pair_s, pair_r,
    a1_s, a1_r, a2_s, a2_r, a2f_r, a3_r, b1_s, b1_r, b2_s, b2_r, b2f_r, sib_s, sib_r,
    sz_s, sz_r, sy_s, sy_r, w_s, w_r, ss_s, ss_r, ge_s, ge_r, ga_s, ga_r,
    ra1_s, ra1_r, ra2_s, ra2_r, rb1_s, rb1_r, rb2_s, rb2_r,
):
    v = lax.axis_index("vocab")
    y, z, c = v // (NZ * NC), (v // NC) % NZ, v % NC
    zz, own = z // N, z % N
    hs2, ht2 = hs // 2, ht // 2
    sa, ta = SPLIT_S, SPLIT_T
    ga = SPLIT_G
    gb = hs2 - ga
    ha, hb = wide_half(ga), wide_half(gb)
    widths = ((sa, hs2 - sa), (ta, ht2 - ta))

    def dev(dy, dz, dc):
        return {"vocab": (((y + dy) % NY) * NZ + (z + dz) % NZ) * NC + (c + dc) % NC}

    def rcopy(src, dst, ssem, rsem, device):
        return pltpu.make_async_remote_copy(
            src_ref=src, dst_ref=dst, send_sem=ssem, recv_sem=rsem,
            device_id=device, device_id_type=MESH,
        )

    load_s = pltpu.make_async_copy(ws_hbm, ws, load_sem.at[0])
    load_t = pltpu.make_async_copy(wt_hbm, wt, load_sem.at[1])
    load_s.start()
    load_t.start()

    barrier = pltpu.get_barrier_semaphore()
    partners = [(0, k, 0) for k in range(1, NZ)]
    partners += [(0, k, 1) for k in range(1, NZ)]
    partners += [(j, 0, d) for j in range(1, NY) for d in range(NC)] + [(0, 0, 1)]
    for p in partners:
        pl.semaphore_signal(barrier, inc=1, device_id=dev(*p), device_id_type=MESH)
    xf[:, :hs2] = sh_ref[:, pl.ds(pl.multiple_of((1 - c) * hs2, 128), hs2)].astype(jnp.float32)
    xf[:, hs2:] = th_ref[:, pl.ds(pl.multiple_of((1 - c) * ht2, 128), ht2)].astype(jnp.float32)
    pl.semaphore_wait(barrier, len(partners))
    pair = rcopy(xf, xg, pair_s, pair_r, dev(0, 0, 1))
    pair.start()

    seg = jnp.broadcast_to(seg_ref[...].astype(jnp.float32), (128, N * ROWS))
    val = jnp.broadcast_to(valid_ref[...].astype(jnp.float32), (128, N * ROWS))
    seg_c, val_c = jnp.transpose(seg)[:, :1], jnp.transpose(val)[:, :1]
    same = jnp.where(seg_c == seg[:1, :], val[:1, :], 0.0)
    count = jnp.sum(same, axis=1, keepdims=True)
    weight = LOSS_SCALE * val_c / jnp.maximum(count, 1.0)
    wcol[...] = jnp.broadcast_to(weight, (N * ROWS, 128)).reshape(NY, HZ, N, BLK, 128)

    pair.wait()

    def put(col, width, full, part):
        mine = full[:, pl.ds(pl.multiple_of(c * width, 128), width)].astype(jnp.float32)
        both = jnp.concatenate(
            [jnp.where(c == 0, mine, part), jnp.where(c == 0, part, mine)], axis=0
        )
        x[own, y, zz, :, pl.ds(pl.multiple_of(col + c * width, 128), width)] = both.astype(
            jnp.bfloat16
        )

    put(0, hs2, sh_ref, xg[:, :hs2])
    put(hs, ht2, th_ref, xg[:, hs2:])

    def cols(u, order, core):
        start = (core * hs2, hs + core * ht2)[u] + (0 if order == 0 else widths[u][0])
        return pl.ds(pl.multiple_of(start, 128), widths[u][order])

    def span(u, core):
        start, width = ((core * hs2, hs2), (hs + core * ht2, ht2))[u]
        return pl.ds(pl.multiple_of(start, 128), width)

    def loop(lo, hi, body):
        def step(i, carry):
            body(i)
            return carry

        lax.fori_loop(lo, hi, step, 0)

    def a1(u, k, ahead):
        source = (z - k + NZ) % NZ
        h, b = source % N, source // N
        block = x.at[h, y, b, :, cols(u, 0, c)]
        return rcopy(block, block, a1_s.at[u], a1_r.at[h, u, b], dev(0, ahead, 0))

    onward, back_y = jnp.where(c == 0, 1, NY - 1), jnp.where(c == 0, NY - 1, 1)

    def a2_on(h, u, b, late):
        block = x.at[h, y, b, :, cols(u, 0, c)]
        return rcopy(block, block, a2_s.at[u], a2f_r.at[u, late], dev(onward, 0, 0))

    def a2_back(h, u, b):
        block = x.at[h, y, b, :, cols(u, 0, c)]
        return rcopy(block, block, a2_s.at[u], a2_r.at[h, u], dev(back_y, 0, 0))

    def a3(u, k):
        source = (z - k + NZ) % NZ
        h, b = source % N, source // N
        block = x.at[h, (y + back_y) % NY, b, :, cols(u, 0, c)]
        return rcopy(block, block, a2_s.at[u], a3_r.at[h, u], dev(onward, 0, 0))

    def b1(h, u, j):
        block = x.at[h, y, zz, :, cols(u, 1, c)]
        return rcopy(block, block, b1_s.at[u], b1_r.at[u], dev(j, 0, 0))

    def b2(u, k, ahead, sem):
        source = (z - k + NZ) % NZ
        block = x.at[source % N, :, source // N, :, cols(u, 1, c)]
        return rcopy(block, block, b2_s.at[u], sem, dev(0, ahead, 0))

    def sib_a(h, u, dy):
        block = x.at[h, (y + dy) % NY, :, :, cols(u, 0, c)]
        return rcopy(block, block, sib_s.at[u], sib_r.at[h, u], dev(0, 0, 1))

    def sib_b(h, u):
        block = x.at[h, :, :, :, cols(u, 1, c)]
        return rcopy(block, block, sib_s.at[u], sib_r.at[h, u], dev(0, 0, 1))

    flat = x.reshape(N * ROWS, hs + ht)

    def arrived(sem, rows, width):
        some = flat.at[pl.ds(0, rows), pl.ds(0, width)]
        pltpu.make_async_copy(some, some, sem).wait()

    def arrived_f32(sem, like):
        pltpu.make_async_copy(like, like, sem).wait()

    def near_first(k0, count, step, body):
        def some(i):
            k = k0 + step * (i // 2)
            body(jnp.where(i % 2 == 0, k, NZ - k))

        loop(0, count, some)

    def behind(h, body):
        near_first(
            jnp.where(own == h, 2, 1), jnp.where(own == h, HZ - 1, HZ), N, body
        )

    ahead = behind

    def send_first(u):
        loop(1, NY, lambda j: b1(own, u, j).start())
        a1(u, 0, 1).start()
        a1(u, 0, NZ - 1).start()
        a2_on(own, u, zz, 0).start()
        a2_back(own, u, zz).start()
        a1(u, 0, 2).start()
        a1(u, 0, NZ - 2).start()

    direct, relayed = (1, NZ - 1, 2, NZ - 2), (3, NZ - 3, 4)

    def relay(u, late):
        for k in (direct, relayed)[late]:
            source = (z - k + NZ) % NZ
            h, b = source % N, source // N
            arrived(a1_r.at[h, u, b], BLK, widths[u][0])
            if k == 2:
                a1(u, k, 1).start()

                @pl.when(c == 0)
                def _():
                    a1(u, k, 2).start()

            if k == NZ - 2:
                a1(u, k, NZ - 1).start()

                @pl.when(c == 1)
                def _():
                    a1(u, k, NZ - 2).start()

            a2_on(h, u, b, late).start()
            a2_back(h, u, b).start()

    def relay_b(u):
        arrived(b1_r.at[u], (NY - 1) * BLK, widths[u][1])
        b2(u, 0, 2, b2f_r.at[u, 0]).start()
        b2(u, 0, NZ - 2, b2f_r.at[u, 1]).start()
        b2(u, 0, 1, b2_r.at[u]).start()
        b2(u, 0, NZ - 1, b2_r.at[u]).start()

    def relay_b2(u):
        arrived(b2f_r.at[u, 0], NY * BLK, widths[u][1])
        b2(u, 2, 1, b2_r.at[u]).start()

        @pl.when(c == 0)
        def _():
            b2(u, 2, 2, b2_r.at[u]).start()

        arrived(b2f_r.at[u, 1], NY * BLK, widths[u][1])
        b2(u, NZ - 2, NZ - 1, b2_r.at[u]).start()

        @pl.when(c == 1)
        def _():
            b2(u, NZ - 2, NZ - 2, b2_r.at[u]).start()

    def relay_y(u, late):
        ks = ((0,) + direct, relayed)[late]
        arrived(a2f_r.at[u, late], len(ks) * BLK, widths[u][0])
        for k in ks:
            a3(u, k).start()
        if late:
            for h in range(N):
                sib_a(h, u, back_y).start()

    def send_sibling_own(u):
        for h in range(N):
            sib_a(h, u, 0).start()

    def send_sibling_b(u):
        arrived(b2_r.at[u], 5 * NY * BLK, widths[u][1])
        for h in range(N):
            sib_b(h, u).start()

    def send_sibling_a(h, u):
        arrived(a2_r.at[h, u], HZ * BLK, widths[u][0])
        sib_a(h, u, onward).start()

    def send_sibling_last(h, u):
        arrived(a3_r.at[h, u], HZ * BLK, widths[u][0])
        sib_a(h, u, 2).start()

    def gathered(u):
        for h in range(N):
            arrived(sib_r.at[h, u], ROWS, (hs2, ht2)[u])

    def student(core, add):
        def tile(i):
            at = pl.ds(pl.multiple_of(i * vs, 128), vs)
            rows = x[:, :, :, :, span(0, core)].reshape(N * ROWS, hs2)
            logits = jnp.dot(rows, ws[span(0, core), at], preferred_element_type=jnp.float32)
            logits = logits.reshape(N, ROWS, vs)
            logit_s[:, :, at] = logit_s[:, :, at] + logits if add else logits

        tile(0)

    def teacher():
        rows = x[:, :, :, :, hs:].reshape(N * ROWS, ht)
        logits = jnp.dot(rows, wt[...], preferred_element_type=jnp.float32)
        logit_t[...] = logits.reshape(N, ROWS, vs)

    lane = lax.broadcasted_iota(jnp.int32, (1, 128), 1)

    def groups(body):
        def some(i):
            for n in range(GROUP // PART):
                body(pl.ds(pl.multiple_of(i * GROUP + n * PART, PART), PART))

        loop(0, ROWS // GROUP, some)

    def stats_s(h):
        def some(at):
            s = logit_s[h, at, :]
            peak = jnp.max(s, axis=1, keepdims=True)
            e = jnp.exp(s - peak)
            exp_s[h, at, :] = e
            total = jnp.sum(e, axis=1, keepdims=True)
            stat_col[h, at, :] = jnp.where(lane == 0, peak, jnp.where(lane == 1, total, 0.0))

        groups(some)

    def stats_t(h):
        def some(at):
            t = logit_t[h, at, :]
            peak = jnp.max(t, axis=1, keepdims=True)
            total = jnp.sum(jnp.exp(t - peak), axis=1, keepdims=True)
            cross = jnp.sum(exp_s[h, at, :] * (logit_s[h, at, :] - t), axis=1, keepdims=True)
            packed = stat_col[h, at, :]
            mean = cross / packed[:, 1:2]
            for m, value in enumerate((cross, peak, total, mean)):
                packed = jnp.where(lane == m + 2, value, packed)
            stat_col[h, at, :] = packed

        groups(some)

    def sz(h, k):
        return rcopy(stat_own.at[h], stat_z.at[h, k], sz_s, sz_r.at[h], dev(0, k, 0))

    def sy(h, n):
        j, d = n // NC, n % NC
        return rcopy(stat_mid.at[h], stat_y.at[h, n], sy_s, sy_r.at[h], dev(j, 0, d))

    def merge(blocks):
        peak_s = functools.reduce(jnp.maximum, [b[0:1] for b in blocks])
        peak_t = functools.reduce(jnp.maximum, [b[3:4] for b in blocks])
        sum_s = cross = sum_t = 0.0
        for b in blocks:
            scale = jnp.exp(b[0:1] - peak_s)
            sum_s = sum_s + scale * b[1:2]
            cross = cross + scale * b[2:3]
            sum_t = sum_t + jnp.exp(b[3:4] - peak_t) * b[4:5]
        return peak_s, sum_s, cross, peak_t, sum_t

    def to_sibling(src, dst, ssem, rsem):
        return rcopy(src, dst, ssem, rsem, dev(0, 0, 1))

    def stats_sib(h):
        return to_sibling(stat_own.at[h], stat_sib.at[h], ss_s, ss_r.at[h])

    def stats_z(h):
        stat_own[h] = jnp.transpose(stat_col[h])[:8, :]
        stats_sib(h).start()
        loop(1, NZ, lambda k: sz(h, k).start())

    def stats_y(h):
        arrived_f32(sz_r.at[h], stat_z.at[h, pl.ds(1, NZ - 1)])
        rows = merge([stat_own[h]] + [stat_z[h, k] for k in range(1, NZ)])
        stat_mid[h] = jnp.concatenate(list(rows) + [jnp.zeros((3, ROWS), jnp.float32)], axis=0)
        loop(1, NY * NC, lambda n: sy(h, n).start())

    def factors(h):
        arrived_f32(sy_r.at[h], stat_y.at[h, pl.ds(1, NY * NC - 1)])
        peak_s, sum_s, cross, peak_t, sum_t = merge(
            [stat_mid[h]] + [stat_y[h, n] for n in range(1, NY * NC)]
        )
        lse_s, lse_t = peak_s + jnp.log(sum_s), peak_t + jnp.log(sum_t)
        kl = cross / sum_s - lse_s + lse_t
        offset = lse_s - lse_t + kl
        stats_sib(h).wait_recv()
        both = []
        for stat in (stat_own[h], stat_sib[h]):
            both += [jnp.exp(stat[0:1] - lse_s), offset - stat[5:6]]
        packed = jnp.concatenate(both + [kl, jnp.zeros((123, ROWS), jnp.float32)], axis=0)
        fac[h] = jnp.transpose(packed)

    def e_sib():
        return to_sibling(e_rows, e_in, ge_s, ge_r)

    def a_sib(h):
        return to_sibling(a_rows.at[h], a_in.at[h], ga_s, ga_r.at[h])

    def head_sib():
        return to_sibling(ws.at[span(0, 1 - c)], w_in, w_s, w_r)

    def grads_e():
        for h in range(N):
            def some(at):
                e_rows[h, at, :] = exp_s[h, at, :].astype(jnp.bfloat16)

            groups(some)
        e_sib().start()

    def grads_a(h):
        def some(at):
            ratio = logit_s[h, at, :] - logit_t[h, at, :]
            a = exp_s[h, at, :] * (ratio - stat_col[h, at, 5:6])
            a_rows[h, at, :] = a.astype(jnp.bfloat16)

        groups(some)
        a_sib(h).start()

    part = hs2 // 2

    def transpose(n, src, start):
        def block(i):
            at = pl.ds(pl.multiple_of(i * TILE, TILE), TILE)
            rows = pl.ds(pl.multiple_of(start + i * TILE, TILE), TILE)
            wst[n, :, at] = jnp.transpose(src[rows, :])

        loop(0, hs2 // TILE, block)

    def back_e(h, n):
        rows = (e_rows, e_in)[n][h]
        sum_e[n, h] = jnp.dot(rows, wst[n], preferred_element_type=jnp.float32)

    def back_a(h, n):
        def block(i):
            at = pl.ds(pl.multiple_of(i * hs2, 128), hs2)
            rows = (a_rows, a_in)[n][h]
            sum_a[n, h, :, at] = jnp.dot(rows, wst[n, :, at], preferred_element_type=jnp.float32)

        block(0)

    def ra1(h, j):
        return rcopy(
            r1.at[h, (y + j) % NY, :, :, pl.ds(0, ga)], ra.at[h, j],
            ra1_s, ra1_r.at[h], dev(j, 0, 0),
        )

    def rb1(h, k):
        return rcopy(
            r1.at[h, :, ((z + k) % NZ) // N, :, pl.ds(ga, gb)], rb.at[h, k],
            rb1_s, rb1_r, dev(0, k, 0),
        )

    def rra2(h, k, d):
        return rcopy(
            r2a.at[h, (c + d) % NC, ((z + k) % NZ) // N], ra2.at[d, k],
            ra2_s, ra2_r, dev(0, k, d),
        )

    def rrb2(h, j, d):
        return rcopy(
            r2b.at[(c + d) % NC, (y + j) % NY], rb2.at[d, j],
            rb2_s, rb2_r, dev(j, 0, d),
        )

    def by_core(total):
        width = total.shape[-1]
        half = wide_half(width)
        fill = jnp.zeros(total.shape[:1] + (8, 2 * half - width), jnp.float32)
        packed = []
        for rows in (total[:, :8], total[:, 8:]):
            right = rows[..., half:]
            if 2 * half > width:
                right = jnp.concatenate([right, fill], axis=2)
            packed.append(jnp.concatenate([rows[..., :half], right], axis=1).astype(jnp.bfloat16))
        return packed

    def reduce_first(h):
        w = wcol[:, :, h, :, 0:1].reshape(ROWS, 1)
        f = [fac[h, :, n:n + 1] for n in range(4)]
        for i in range(2):
            at = slice(i * part, (i + 1) * part)
            total = 0.0
            for n in range(2):
                some = sum_a[n, h, :, at] - f[2 * n + 1] * sum_e[n, h, :, at]
                total = total + (f[2 * n] * w) * some
            r1[h, :, :, :, at] = total.astype(jnp.bfloat16).reshape(NY, HZ, BLK, part)
        loop(1, NY, lambda j: ra1(h, j).start())
        ahead(h, lambda k: rb1(h, k).start())

    def reduce_second(h):
        arrived(ra1_r.at[h], (NY - 1) * HZ * BLK, ga)
        total = r1[h, y, :, :, :ga].astype(jnp.float32)
        for j in range(1, NY):
            total = total + ra[h, j].astype(jnp.float32)
        for d, rows in enumerate(by_core(total)):
            r2a[h, d] = rows

        def give(k):
            rra2(h, k, 0).start()
            rra2(h, k, 1).start()

        ahead(h, give)

        @pl.when(own == h)
        def _():
            arrived(rb1_r, (NZ - 1) * NY * BLK, gb)
            total = r1[h, :, zz, :, ga:].astype(jnp.float32)
            for k in range(1, NZ):
                total = total + rb[h, k].astype(jnp.float32)
            for d, rows in enumerate(by_core(total)):
                r2b[d] = rows
            rra2(h, 0, 1).start()
            loop(1, 2 * NY, lambda n: rrb2(h, n // 2, n % 2).start())

    def final(h):
        @pl.when(own == h)
        def _():
            arrived(ra2_r, (2 * NZ - 1) * BLK, ha)
            arrived(rb2_r, (2 * NY - 1) * BLK, hb)
            for d in range(NC):
                left = (ra2[d, 0] if d else r2a[h, c, zz]).astype(jnp.float32)
                for k in range(1, NZ):
                    left = left + ra2[d, k].astype(jnp.float32)
                right = (rb2[d, 0] if d else r2b[c, y]).astype(jnp.float32)
                for j in range(1, NY):
                    right = right + rb2[d, j].astype(jnp.float32)
                start = 0
                for some, width in ((left, ga), (right, gb)):
                    half = some.shape[-1]
                    for rows, some_width in ((some[:8], half), (some[8:], width - half)):
                        at = pl.multiple_of(((c + d) % NC) * hs2 + start, 128)
                        out_ref[:, pl.ds(at, some_width)] = rows[:, :some_width]
                        start += some_width
            at = pl.multiple_of((y * HZ + zz) * BLK + c * 8, 8)
            kl = fac[h, pl.ds(at, 8), 4:5]
            row = lax.broadcasted_iota(jnp.int32, (8, 128), 0)
            col = lax.broadcasted_iota(jnp.int32, (8, 128), 1)
            kl = jnp.sum(jnp.where(row == col, kl, 0.0), axis=0, keepdims=True)
            out_ref[:, hs:] = jnp.broadcast_to(kl, (8, 128))

    def gather_left():
        for u in range(2):
            arrived(a1_s.at[u], (NZ - 1) * BLK, widths[u][0])
            arrived(b1_s.at[u], (NY - 1) * BLK, widths[u][1])
            arrived(b2_s.at[u], (NZ - 1) * NY * BLK, widths[u][1])
            arrived(a2_s.at[u], (NY - 1) * N * HZ * BLK, widths[u][0])
            arrived(sib_s.at[u], N * ROWS, (hs2, ht2)[u])

    def rest_left():
        arrived_f32(sz_s, stat_z.at[:, pl.ds(1, NZ - 1)])
        arrived_f32(sy_s, stat_y.at[:, pl.ds(1, NY * NC - 1)])
        head_sib().wait_send()
        arrived_f32(ss_s, stat_sib)
        arrived_f32(ge_s, e_rows)
        arrived_f32(ga_s, a_rows)
        arrived(ra1_s, N * (NY - 1) * HZ * BLK, ga)
        arrived(rb1_s, (NZ - 1) * NY * BLK, gb)
        arrived(ra2_s, (2 * NZ - 1) * BLK, ha)
        arrived(rb2_s, (2 * NY - 1) * BLK, hb)

    send_first(0)
    load_s.wait()
    head_sib().start()
    transpose(0, ws, c * hs2)
    send_first(1)
    relay_b(0)
    relay(0, 0)
    relay_b(1)
    relay(1, 0)
    relay(0, 1)
    relay_b2(0)
    send_sibling_own(0)
    relay_y(0, 0)
    relay(1, 1)
    relay_y(0, 1)
    relay_b2(1)
    send_sibling_own(1)
    relay_y(1, 0)
    head_sib().wait_recv()
    transpose(1, w_in, 0)
    relay_y(1, 1)
    load_t.wait()
    for h in range(N):
        send_sibling_a(h, 0)
    send_sibling_b(0)
    for h in range(N):
        send_sibling_last(h, 0)
    student(c, False)
    gathered(0)
    student(1 - c, True)
    for h in range(N):
        send_sibling_a(h, 1)
    send_sibling_b(1)
    for h in range(N):
        stats_s(h)
    for h in range(N):
        send_sibling_last(h, 1)
    grads_e()
    gathered(1)
    teacher()
    for h in range(N):
        stats_t(h)
        stats_z(h)
    for h in range(N):
        grads_a(h)
    back_e(0, 0)
    back_a(0, 0)
    stats_y(0)
    e_sib().wait_recv()
    back_e(0, 1)
    stats_y(1)
    a_sib(0).wait_recv()
    back_a(0, 1)
    back_e(1, 0)
    factors(0)
    reduce_first(0)
    back_e(1, 1)
    back_a(1, 0)
    a_sib(1).wait_recv()
    back_a(1, 1)
    factors(1)
    reduce_first(1)
    reduce_second(0)
    gather_left()
    reduce_second(1)
    for h in range(N):
        final(h)
    rest_left()


def split(result_ref, kl_ref, grad_ref):
    rows, hs = grad_ref.shape
    kl_ref[...] = result_ref[:1, hs:hs + rows]
    grad_ref[...] = result_ref[:, :hs].astype(jnp.bfloat16)


def local(student_hidden, teacher_hidden, student_head, teacher_head, segment_ids, valid_mask):
    rows, hs = student_hidden.shape
    ht = teacher_hidden.shape[1]
    vs = student_head.shape[1]
    tokens = segment_ids.shape[0]
    hs2 = hs // 2
    ga, gb = SPLIT_G, hs2 - SPLIT_G
    ha, hb = wide_half(ga), wide_half(gb)
    f32, bf16 = jnp.float32, jnp.bfloat16
    dma = pltpu.SemaphoreType.DMA
    vmem = pl.BlockSpec(memory_space=pltpu.VMEM)
    hbm = pl.BlockSpec(memory_space=pl.ANY)
    flops = 2 * tokens * vs * (2 * hs + ht)
    result = pl.pallas_call(
        functools.partial(kernel, hs, ht, vs),
        out_shape=jax.ShapeDtypeStruct((rows, hs + 128), f32),
        in_specs=[vmem, vmem, vmem, vmem, hbm, hbm],
        out_specs=vmem,
        scratch_shapes=[
            pltpu.VMEM((hs, vs), bf16),
            pltpu.VMEM((hs2, vs), bf16),
            pltpu.VMEM((2, vs, hs2), bf16),
            pltpu.VMEM((ht, vs), bf16),
            pltpu.VMEM((N, NY, HZ, BLK, hs + ht), bf16),
            pltpu.VMEM((rows, (hs + ht) // 2), f32),
            pltpu.VMEM((rows, (hs + ht) // 2), f32),
            pltpu.VMEM((N, ROWS, vs), f32),
            pltpu.VMEM((N, ROWS, vs), f32),
            pltpu.VMEM((N, ROWS, vs), f32),
            pltpu.VMEM((2, N, ROWS, hs2), f32),
            pltpu.VMEM((2, N, ROWS, hs2), f32),
            pltpu.VMEM((N, ROWS, 128), f32),
            pltpu.VMEM((N, 8, ROWS), f32),
            pltpu.VMEM((N, 8, ROWS), f32),
            pltpu.VMEM((N, NZ, 8, ROWS), f32),
            pltpu.VMEM((N, 8, ROWS), f32),
            pltpu.VMEM((N, NY * NC, 8, ROWS), f32),
            pltpu.VMEM((N, ROWS, 128), f32),
            pltpu.VMEM((NY, HZ, N, BLK, 128), f32),
            pltpu.VMEM((N, ROWS, vs), bf16),
            pltpu.VMEM((N, ROWS, vs), bf16),
            pltpu.VMEM((N, ROWS, vs), bf16),
            pltpu.VMEM((N, ROWS, vs), bf16),
            pltpu.VMEM((N, NY, HZ, BLK, hs2), bf16),
            pltpu.VMEM((N, NY, HZ, BLK, ga), bf16),
            pltpu.VMEM((N, NC, HZ, BLK, ha), bf16),
            pltpu.VMEM((NC, NZ, BLK, ha), bf16),
            pltpu.VMEM((N, NZ, NY, BLK, gb), bf16),
            pltpu.VMEM((NC, NY, BLK, hb), bf16),
            pltpu.VMEM((NC, NY, BLK, hb), bf16),
            dma((2,)), dma(()), dma(()),
            dma((2,)), dma((N, 2, HZ)), dma((2,)), dma((N, 2)), dma((N, 2)), dma((N, 2)),
            dma((2,)), dma((2,)), dma((2,)), dma((2,)), dma((2, 2)),
            dma((2,)), dma((N, 2)),
            dma(()), dma((N,)), dma(()), dma((N,)), dma(()), dma(()), dma(()), dma((N,)),
            dma(()), dma(()), dma(()), dma((N,)),
            dma(()), dma((N,)), dma(()), dma(()),
            dma(()), dma(()), dma(()), dma(()),
        ],
        compiler_params=pltpu.CompilerParams(
            collective_id=0, has_side_effects=True, vmem_limit_bytes=60 * 1024 * 1024
        ),
        cost_estimate=pl.CostEstimate(
            flops=flops, bytes_accessed=2 * vs * (hs + ht), transcendentals=2 * tokens * vs
        ),
    )(
        student_hidden, teacher_hidden,
        segment_ids.reshape(1, tokens), valid_mask.reshape(1, tokens),
        student_head, teacher_head,
    )
    kl, grad = pl.pallas_call(
        split,
        out_shape=(jax.ShapeDtypeStruct((1, rows), f32), jax.ShapeDtypeStruct((rows, hs), bf16)),
        in_specs=[vmem],
        out_specs=(vmem, vmem),
    )(result)
    return kl.reshape(rows), grad


def solution(mesh):
    in_specs = (
        P(("dp", "vocab"), None),
        P(("dp", "vocab"), None),
        P("dp", "vocab"),
        P("dp", "vocab"),
        P("dp"),
        P("dp"),
    )
    out_specs = (P(("dp", "vocab")), P(("dp", "vocab"), None))
    return jax.shard_map(local, mesh=mesh, in_specs=in_specs, out_specs=out_specs, check_vma=False)
```

```python
import functools

import jax
import jax.numpy as jnp
from jax import lax
from jax.experimental import pallas as pl
from jax.experimental.pallas import tpu as pltpu
from jax.sharding import PartitionSpec as P

LOSS_SCALE = 1024.0
NY, NZ, NC = 4, 8, 2
N = 2
HZ = NZ // N
BLK = 16
ROWS = NY * HZ * BLK
TILE = 256
GROUP, PART = 128, 32
SPLIT_S, SPLIT_T, SPLIT_G = 1024, 640, 896
MESH = pl.DeviceIdType.MESH


def wide_half(width):
    return (width + 255) // 256 * 128


def kernel(
    hs, ht, vs,
    sh_ref, th_ref, seg_ref, valid_ref, ws_hbm, wt_hbm,
    out_ref,
    ws, w_in, wst, wt, x, xf, xg, logit_s, logit_t, exp_s,
    sum_e, sum_a, stat_col, stat_own, stat_sib, stat_z, stat_mid, stat_y, fac, wcol,
    e_rows, e_in, a_rows, a_in, r1, ra, r2a, ra2, rb, r2b, rb2,
    load_sem, pair_s, pair_r,
    a1_s, a1_r, a2_s, a2_r, a2f_r, a3_r, b1_s, b1_r, b2_s, b2_r, b2f_r, sib_s, sib_r,
    sz_s, sz_r, sy_s, sy_r, w_s, w_r, ss_s, ss_r, ge_s, ge_r, ga_s, ga_r,
    ra1_s, ra1_r, ra2_s, ra2_r, rb1_s, rb1_r, rb2_s, rb2_r,
):
    v = lax.axis_index("vocab")
    y, z, c = v // (NZ * NC), (v // NC) % NZ, v % NC
    zz, own = z // N, z % N
    hs2, ht2 = hs // 2, ht // 2
    sa, ta = SPLIT_S, SPLIT_T
    ga = SPLIT_G
    gb = hs2 - ga
    ha, hb = wide_half(ga), wide_half(gb)
    widths = ((sa, hs2 - sa), (ta, ht2 - ta))

    def dev(dy, dz, dc):
        return {"vocab": (((y + dy) % NY) * NZ + (z + dz) % NZ) * NC + (c + dc) % NC}

    def rcopy(src, dst, ssem, rsem, device):
        return pltpu.make_async_remote_copy(
            src_ref=src, dst_ref=dst, send_sem=ssem, recv_sem=rsem,
            device_id=device, device_id_type=MESH,
        )

    load_s = pltpu.make_async_copy(ws_hbm, ws, load_sem.at[0])
    load_t = pltpu.make_async_copy(wt_hbm, wt, load_sem.at[1])
    load_s.start()
    load_t.start()

    barrier = pltpu.get_barrier_semaphore()
    partners = [(0, k, 0) for k in range(1, NZ)]
    partners += [(0, k, 1) for k in range(1, NZ)]
    partners += [(j, 0, d) for j in range(1, NY) for d in range(NC)] + [(0, 0, 1)]
    for p in partners:
        pl.semaphore_signal(barrier, inc=1, device_id=dev(*p), device_id_type=MESH)
    xf[:, :hs2] = sh_ref[:, pl.ds(pl.multiple_of((1 - c) * hs2, 128), hs2)].astype(jnp.float32)
    xf[:, hs2:] = th_ref[:, pl.ds(pl.multiple_of((1 - c) * ht2, 128), ht2)].astype(jnp.float32)
    pl.semaphore_wait(barrier, len(partners))
    pair = rcopy(xf, xg, pair_s, pair_r, dev(0, 0, 1))
    pair.start()

    seg = jnp.broadcast_to(seg_ref[...].astype(jnp.float32), (128, N * ROWS))
    val = jnp.broadcast_to(valid_ref[...].astype(jnp.float32), (128, N * ROWS))
    seg_c, val_c = jnp.transpose(seg)[:, :1], jnp.transpose(val)[:, :1]
    same = jnp.where(seg_c == seg[:1, :], val[:1, :], 0.0)
    count = jnp.sum(same, axis=1, keepdims=True)
    weight = LOSS_SCALE * val_c / jnp.maximum(count, 1.0)
    wcol[...] = jnp.broadcast_to(weight, (N * ROWS, 128)).reshape(NY, HZ, N, BLK, 128)

    pair.wait()

    def put(col, width, full, part):
        mine = full[:, pl.ds(pl.multiple_of(c * width, 128), width)].astype(jnp.float32)
        both = jnp.concatenate(
            [jnp.where(c == 0, mine, part), jnp.where(c == 0, part, mine)], axis=0
        )
        x[own, y, zz, :, pl.ds(pl.multiple_of(col + c * width, 128), width)] = both.astype(
            jnp.bfloat16
        )

    put(0, hs2, sh_ref, xg[:, :hs2])
    put(hs, ht2, th_ref, xg[:, hs2:])

    def cols(u, order, core):
        start = (core * hs2, hs + core * ht2)[u] + (0 if order == 0 else widths[u][0])
        return pl.ds(pl.multiple_of(start, 128), widths[u][order])

    def span(u, core):
        start, width = ((core * hs2, hs2), (hs + core * ht2, ht2))[u]
        return pl.ds(pl.multiple_of(start, 128), width)

    def loop(lo, hi, body):
        def step(i, carry):
            body(i)
            return carry

        lax.fori_loop(lo, hi, step, 0)

    def a1(u, k, ahead):
        source = (z - k + NZ) % NZ
        h, b = source % N, source // N
        block = x.at[h, y, b, :, cols(u, 0, c)]
        return rcopy(block, block, a1_s.at[u], a1_r.at[h, u, b], dev(0, ahead, 0))

    onward, back_y = jnp.where(c == 0, 1, NY - 1), jnp.where(c == 0, NY - 1, 1)

    def a2_on(h, u, b, late):
        block = x.at[h, y, b, :, cols(u, 0, c)]
        return rcopy(block, block, a2_s.at[u], a2f_r.at[u, late], dev(onward, 0, 0))

    def a2_back(h, u, b):
        block = x.at[h, y, b, :, cols(u, 0, c)]
        return rcopy(block, block, a2_s.at[u], a2_r.at[h, u], dev(back_y, 0, 0))

    def a3(u, k):
        source = (z - k + NZ) % NZ
        h, b = source % N, source // N
        block = x.at[h, (y + back_y) % NY, b, :, cols(u, 0, c)]
        return rcopy(block, block, a2_s.at[u], a3_r.at[h, u], dev(onward, 0, 0))

    def b1(h, u, j):
        block = x.at[h, y, zz, :, cols(u, 1, c)]
        return rcopy(block, block, b1_s.at[u], b1_r.at[u], dev(j, 0, 0))

    def b2(u, k, ahead, sem):
        source = (z - k + NZ) % NZ
        block = x.at[source % N, :, source // N, :, cols(u, 1, c)]
        return rcopy(block, block, b2_s.at[u], sem, dev(0, ahead, 0))

    def sib_a(h, u, dy):
        block = x.at[h, (y + dy) % NY, :, :, cols(u, 0, c)]
        return rcopy(block, block, sib_s.at[u], sib_r.at[h, u], dev(0, 0, 1))

    def sib_b(h, u):
        block = x.at[h, :, :, :, cols(u, 1, c)]
        return rcopy(block, block, sib_s.at[u], sib_r.at[h, u], dev(0, 0, 1))

    flat = x.reshape(N * ROWS, hs + ht)

    def arrived(sem, rows, width):
        some = flat.at[pl.ds(0, rows), pl.ds(0, width)]
        pltpu.make_async_copy(some, some, sem).wait()

    def arrived_f32(sem, like):
        pltpu.make_async_copy(like, like, sem).wait()

    def near_first(k0, count, step, body):
        def some(i):
            k = k0 + step * (i // 2)
            body(jnp.where(i % 2 == 0, k, NZ - k))

        loop(0, count, some)

    def behind(h, body):
        near_first(
            jnp.where(own == h, 2, 1), jnp.where(own == h, HZ - 1, HZ), N, body
        )

    ahead = behind

    def send_first(u):
        loop(1, NY, lambda j: b1(own, u, j).start())
        a1(u, 0, 1).start()
        a1(u, 0, NZ - 1).start()
        a2_on(own, u, zz, 0).start()
        a2_back(own, u, zz).start()
        a1(u, 0, 2).start()
        a1(u, 0, NZ - 2).start()

    direct, relayed = (1, NZ - 1, 2, NZ - 2), (3, NZ - 3, 4)

    def relay(u, late):
        for k in (direct, relayed)[late]:
            source = (z - k + NZ) % NZ
            h, b = source % N, source // N
            arrived(a1_r.at[h, u, b], BLK, widths[u][0])
            if k == 2:
                a1(u, k, 1).start()

                @pl.when(c == 0)
                def _():
                    a1(u, k, 2).start()

            if k == NZ - 2:
                a1(u, k, NZ - 1).start()

                @pl.when(c == 1)
                def _():
                    a1(u, k, NZ - 2).start()

            a2_on(h, u, b, late).start()
            a2_back(h, u, b).start()

    def relay_b(u):
        arrived(b1_r.at[u], (NY - 1) * BLK, widths[u][1])
        b2(u, 0, 2, b2f_r.at[u, 0]).start()
        b2(u, 0, NZ - 2, b2f_r.at[u, 1]).start()
        b2(u, 0, 1, b2_r.at[u]).start()
        b2(u, 0, NZ - 1, b2_r.at[u]).start()

    def relay_b2(u):
        arrived(b2f_r.at[u, 0], NY * BLK, widths[u][1])
        b2(u, 2, 1, b2_r.at[u]).start()

        @pl.when(c == 0)
        def _():
            b2(u, 2, 2, b2_r.at[u]).start()

        arrived(b2f_r.at[u, 1], NY * BLK, widths[u][1])
        b2(u, NZ - 2, NZ - 1, b2_r.at[u]).start()

        @pl.when(c == 1)
        def _():
            b2(u, NZ - 2, NZ - 2, b2_r.at[u]).start()

    def relay_y(u, late):
        ks = ((0,) + direct, relayed)[late]
        arrived(a2f_r.at[u, late], len(ks) * BLK, widths[u][0])
        for k in ks:
            a3(u, k).start()
        if late:
            for h in range(N):
                sib_a(h, u, back_y).start()

    def send_sibling_own(u):
        for h in range(N):
            sib_a(h, u, 0).start()

    def send_sibling_b(u):
        arrived(b2_r.at[u], 5 * NY * BLK, widths[u][1])
        for h in range(N):
            sib_b(h, u).start()

    def send_sibling_a(h, u):
        arrived(a2_r.at[h, u], HZ * BLK, widths[u][0])
        sib_a(h, u, onward).start()

    def send_sibling_last(h, u):
        arrived(a3_r.at[h, u], HZ * BLK, widths[u][0])
        sib_a(h, u, 2).start()

    def gathered(u):
        for h in range(N):
            arrived(sib_r.at[h, u], ROWS, (hs2, ht2)[u])

    def student(core, add):
        def tile(i):
            at = pl.ds(pl.multiple_of(i * vs, 128), vs)
            rows = x[:, :, :, :, span(0, core)].reshape(N * ROWS, hs2)
            logits = jnp.dot(rows, ws[span(0, core), at], preferred_element_type=jnp.float32)
            logits = logits.reshape(N, ROWS, vs)
            logit_s[:, :, at] = logit_s[:, :, at] + logits if add else logits

        tile(0)

    def teacher():
        rows = x[:, :, :, :, hs:].reshape(N * ROWS, ht)
        logits = jnp.dot(rows, wt[...], preferred_element_type=jnp.float32)
        logit_t[...] = logits.reshape(N, ROWS, vs)

    lane = lax.broadcasted_iota(jnp.int32, (1, 128), 1)

    def groups(body):
        def some(i):
            for n in range(GROUP // PART):
                body(pl.ds(pl.multiple_of(i * GROUP + n * PART, PART), PART))

        loop(0, ROWS // GROUP, some)

    def stats_s(h):
        def some(at):
            s = logit_s[h, at, :]
            peak = jnp.max(s, axis=1, keepdims=True)
            e = jnp.exp(s - peak)
            exp_s[h, at, :] = e
            e_rows[h, at, :] = e.astype(jnp.bfloat16)
            total = jnp.sum(e, axis=1, keepdims=True)
            stat_col[h, at, :] = jnp.where(lane == 0, peak, jnp.where(lane == 1, total, 0.0))

        groups(some)

    def stats_t(h):
        def some(at):
            t = logit_t[h, at, :]
            peak = jnp.max(t, axis=1, keepdims=True)
            total = jnp.sum(jnp.exp(t - peak), axis=1, keepdims=True)
            cross = jnp.sum(exp_s[h, at, :] * (logit_s[h, at, :] - t), axis=1, keepdims=True)
            packed = stat_col[h, at, :]
            mean = cross / packed[:, 1:2]
            for m, value in enumerate((cross, peak, total, mean)):
                packed = jnp.where(lane == m + 2, value, packed)
            stat_col[h, at, :] = packed

        groups(some)

    def sz(h, k):
        return rcopy(stat_own.at[h], stat_z.at[h, k], sz_s, sz_r.at[h], dev(0, k, 0))

    def sy(h, n):
        j, d = n // NC, n % NC
        return rcopy(stat_mid.at[h], stat_y.at[h, n], sy_s, sy_r.at[h], dev(j, 0, d))

    def merge(blocks):
        peak_s = functools.reduce(jnp.maximum, [b[0:1] for b in blocks])
        peak_t = functools.reduce(jnp.maximum, [b[3:4] for b in blocks])
        sum_s = cross = sum_t = 0.0
        for b in blocks:
            scale = jnp.exp(b[0:1] - peak_s)
            sum_s = sum_s + scale * b[1:2]
            cross = cross + scale * b[2:3]
            sum_t = sum_t + jnp.exp(b[3:4] - peak_t) * b[4:5]
        return peak_s, sum_s, cross, peak_t, sum_t

    def to_sibling(src, dst, ssem, rsem):
        return rcopy(src, dst, ssem, rsem, dev(0, 0, 1))

    def stats_sib(h):
        return to_sibling(stat_own.at[h], stat_sib.at[h], ss_s, ss_r.at[h])

    def stats_z(h):
        stat_own[h] = jnp.transpose(stat_col[h])[:8, :]
        stats_sib(h).start()
        loop(1, NZ, lambda k: sz(h, k).start())

    def stats_y(h):
        arrived_f32(sz_r.at[h], stat_z.at[h, pl.ds(1, NZ - 1)])
        rows = merge([stat_own[h]] + [stat_z[h, k] for k in range(1, NZ)])
        stat_mid[h] = jnp.concatenate(list(rows) + [jnp.zeros((3, ROWS), jnp.float32)], axis=0)
        loop(1, NY * NC, lambda n: sy(h, n).start())

    def factors(h):
        arrived_f32(sy_r.at[h], stat_y.at[h, pl.ds(1, NY * NC - 1)])
        peak_s, sum_s, cross, peak_t, sum_t = merge(
            [stat_mid[h]] + [stat_y[h, n] for n in range(1, NY * NC)]
        )
        lse_s, lse_t = peak_s + jnp.log(sum_s), peak_t + jnp.log(sum_t)
        kl = cross / sum_s - lse_s + lse_t
        offset = lse_s - lse_t + kl
        stats_sib(h).wait_recv()
        both = []
        for stat in (stat_own[h], stat_sib[h]):
            both += [jnp.exp(stat[0:1] - lse_s), offset - stat[5:6]]
        packed = jnp.concatenate(both + [kl, jnp.zeros((123, ROWS), jnp.float32)], axis=0)
        fac[h] = jnp.transpose(packed)

    def e_sib():
        return to_sibling(e_rows, e_in, ge_s, ge_r)

    def a_sib(h):
        return to_sibling(a_rows.at[h], a_in.at[h], ga_s, ga_r.at[h])

    def head_sib():
        return to_sibling(ws.at[span(0, 1 - c)], w_in, w_s, w_r)

    def grads_a(h):
        def some(at):
            ratio = logit_s[h, at, :] - logit_t[h, at, :]
            a = exp_s[h, at, :] * (ratio - stat_col[h, at, 5:6])
            a_rows[h, at, :] = a.astype(jnp.bfloat16)

        groups(some)
        a_sib(h).start()

    part = hs2 // 2

    def transpose(n, src, start):
        def block(i):
            at = pl.ds(pl.multiple_of(i * TILE, TILE), TILE)
            rows = pl.ds(pl.multiple_of(start + i * TILE, TILE), TILE)
            wst[n, :, at] = jnp.transpose(src[rows, :])

        loop(0, hs2 // TILE, block)

    def back_e(h, n):
        rows = (e_rows, e_in)[n][h]
        sum_e[n, h] = jnp.dot(rows, wst[n], preferred_element_type=jnp.float32)

    def back_a(h, n):
        def block(i):
            at = pl.ds(pl.multiple_of(i * hs2, 128), hs2)
            rows = (a_rows, a_in)[n][h]
            sum_a[n, h, :, at] = jnp.dot(rows, wst[n, :, at], preferred_element_type=jnp.float32)

        block(0)

    def ra1(h, j, start, width):
        at = pl.ds(start, width)
        return rcopy(
            r1.at[h, (y + j) % NY, :, :, at], ra.at[h, j, :, :, at],
            ra1_s, ra1_r.at[h], dev(j, 0, 0),
        )

    def rb1(h, k):
        return rcopy(
            r1.at[h, :, ((z + k) % NZ) // N, :, pl.ds(ga, gb)], rb.at[h, k],
            rb1_s, rb1_r, dev(0, k, 0),
        )

    def rra2(h, k, d):
        return rcopy(
            r2a.at[h, (c + d) % NC, ((z + k) % NZ) // N], ra2.at[d, k],
            ra2_s, ra2_r, dev(0, k, d),
        )

    def rrb2(h, j, d):
        return rcopy(
            r2b.at[(c + d) % NC, (y + j) % NY], rb2.at[d, j],
            rb2_s, rb2_r, dev(j, 0, d),
        )

    def by_core(total):
        width = total.shape[-1]
        half = wide_half(width)
        fill = jnp.zeros(total.shape[:1] + (8, 2 * half - width), jnp.float32)
        packed = []
        for rows in (total[:, :8], total[:, 8:]):
            right = rows[..., half:]
            if 2 * half > width:
                right = jnp.concatenate([right, fill], axis=2)
            packed.append(jnp.concatenate([rows[..., :half], right], axis=1).astype(jnp.bfloat16))
        return packed

    def reduce_first(h):
        w = wcol[:, :, h, :, 0:1].reshape(ROWS, 1)
        f = [fac[h, :, n:n + 1] for n in range(4)]
        for i in range(2):
            at = slice(i * part, (i + 1) * part)
            total = 0.0
            for n in range(2):
                some = sum_a[n, h, :, at] - f[2 * n + 1] * sum_e[n, h, :, at]
                total = total + (f[2 * n] * w) * some
            r1[h, :, :, :, at] = total.astype(jnp.bfloat16).reshape(NY, HZ, BLK, part)
            start, width = (0, part) if i == 0 else (part, ga - part)
            loop(1, NY, lambda j, start=start, width=width: ra1(h, j, start, width).start())
        ahead(h, lambda k: rb1(h, k).start())

    def reduce_second(h):
        arrived(ra1_r.at[h], (NY - 1) * HZ * BLK, ga)
        total = r1[h, y, :, :, :ga].astype(jnp.float32)
        for j in range(1, NY):
            total = total + ra[h, j].astype(jnp.float32)
        for d, rows in enumerate(by_core(total)):
            r2a[h, d] = rows

        def give(k):
            rra2(h, k, 0).start()
            rra2(h, k, 1).start()

        ahead(h, give)

        @pl.when(own == h)
        def _():
            arrived(rb1_r, (NZ - 1) * NY * BLK, gb)
            total = r1[h, :, zz, :, ga:].astype(jnp.float32)
            for k in range(1, NZ):
                total = total + rb[h, k].astype(jnp.float32)
            for d, rows in enumerate(by_core(total)):
                r2b[d] = rows
            rra2(h, 0, 1).start()
            loop(1, 2 * NY, lambda n: rrb2(h, n // 2, n % 2).start())

    def final(h):
        @pl.when(own == h)
        def _():
            arrived(ra2_r, (2 * NZ - 1) * BLK, ha)
            arrived(rb2_r, (2 * NY - 1) * BLK, hb)
            for d in range(NC):
                left = (ra2[d, 0] if d else r2a[h, c, zz]).astype(jnp.float32)
                for k in range(1, NZ):
                    left = left + ra2[d, k].astype(jnp.float32)
                right = (rb2[d, 0] if d else r2b[c, y]).astype(jnp.float32)
                for j in range(1, NY):
                    right = right + rb2[d, j].astype(jnp.float32)
                start = 0
                for some, width in ((left, ga), (right, gb)):
                    half = some.shape[-1]
                    for rows, some_width in ((some[:8], half), (some[8:], width - half)):
                        at = pl.multiple_of(((c + d) % NC) * hs2 + start, 128)
                        out_ref[:, pl.ds(at, some_width)] = rows[:, :some_width]
                        start += some_width
            at = pl.multiple_of((y * HZ + zz) * BLK + c * 8, 8)
            kl = fac[h, pl.ds(at, 8), 4:5]
            row = lax.broadcasted_iota(jnp.int32, (8, 128), 0)
            col = lax.broadcasted_iota(jnp.int32, (8, 128), 1)
            kl = jnp.sum(jnp.where(row == col, kl, 0.0), axis=0, keepdims=True)
            out_ref[:, hs:] = jnp.broadcast_to(kl, (8, 128))

    def gather_left():
        for u in range(2):
            arrived(a1_s.at[u], (NZ - 1) * BLK, widths[u][0])
            arrived(b1_s.at[u], (NY - 1) * BLK, widths[u][1])
            arrived(b2_s.at[u], (NZ - 1) * NY * BLK, widths[u][1])
            arrived(a2_s.at[u], (NY - 1) * N * HZ * BLK, widths[u][0])
            arrived(sib_s.at[u], N * ROWS, (hs2, ht2)[u])

    def rest_left():
        arrived_f32(sz_s, stat_z.at[:, pl.ds(1, NZ - 1)])
        arrived_f32(sy_s, stat_y.at[:, pl.ds(1, NY * NC - 1)])
        head_sib().wait_send()
        arrived_f32(ss_s, stat_sib)
        arrived_f32(ge_s, e_rows)
        arrived_f32(ga_s, a_rows)
        arrived(ra1_s, N * (NY - 1) * HZ * BLK, ga)
        arrived(rb1_s, (NZ - 1) * NY * BLK, gb)
        arrived(ra2_s, (2 * NZ - 1) * BLK, ha)
        arrived(rb2_s, (2 * NY - 1) * BLK, hb)

    send_first(0)
    load_s.wait()
    head_sib().start()
    transpose(0, ws, c * hs2)
    send_first(1)
    relay_b(0)
    relay(0, 0)
    relay_b(1)
    relay(1, 0)
    relay(0, 1)
    relay_b2(0)
    send_sibling_own(0)
    relay_y(0, 0)
    relay(1, 1)
    relay_y(0, 1)
    relay_b2(1)
    send_sibling_own(1)
    relay_y(1, 0)
    head_sib().wait_recv()
    transpose(1, w_in, 0)
    relay_y(1, 1)
    load_t.wait()
    for h in range(N):
        send_sibling_a(h, 0)
    send_sibling_b(0)
    for h in range(N):
        send_sibling_last(h, 0)
    student(c, False)
    gathered(0)
    student(1 - c, True)
    for h in range(N):
        send_sibling_a(h, 1)
    send_sibling_b(1)
    for h in range(N):
        stats_s(h)
    for h in range(N):
        send_sibling_last(h, 1)
    e_sib().start()
    gathered(1)
    teacher()
    for h in range(N):
        stats_t(h)
        stats_z(h)
    for h in range(N):
        grads_a(h)
    back_e(0, 0)
    back_a(0, 0)
    stats_y(0)
    e_sib().wait_recv()
    back_e(0, 1)
    stats_y(1)
    a_sib(0).wait_recv()
    back_a(0, 1)
    back_e(1, 0)
    factors(0)
    reduce_first(0)
    back_e(1, 1)
    back_a(1, 0)
    a_sib(1).wait_recv()
    back_a(1, 1)
    factors(1)
    reduce_first(1)
    reduce_second(0)
    gather_left()
    reduce_second(1)
    for h in range(N):
        final(h)
    rest_left()


def split(result_ref, kl_ref, grad_ref):
    rows, hs = grad_ref.shape
    kl_ref[...] = result_ref[:1, hs:hs + rows]
    grad_ref[...] = result_ref[:, :hs].astype(jnp.bfloat16)


def local(student_hidden, teacher_hidden, student_head, teacher_head, segment_ids, valid_mask):
    rows, hs = student_hidden.shape
    ht = teacher_hidden.shape[1]
    vs = student_head.shape[1]
    tokens = segment_ids.shape[0]
    hs2 = hs // 2
    ga, gb = SPLIT_G, hs2 - SPLIT_G
    ha, hb = wide_half(ga), wide_half(gb)
    f32, bf16 = jnp.float32, jnp.bfloat16
    dma = pltpu.SemaphoreType.DMA
    vmem = pl.BlockSpec(memory_space=pltpu.VMEM)
    hbm = pl.BlockSpec(memory_space=pl.ANY)
    flops = 2 * tokens * vs * (2 * hs + ht)
    result = pl.pallas_call(
        functools.partial(kernel, hs, ht, vs),
        out_shape=jax.ShapeDtypeStruct((rows, hs + 128), f32),
        in_specs=[vmem, vmem, vmem, vmem, hbm, hbm],
        out_specs=vmem,
        scratch_shapes=[
            pltpu.VMEM((hs, vs), bf16),
            pltpu.VMEM((hs2, vs), bf16),
            pltpu.VMEM((2, vs, hs2), bf16),
            pltpu.VMEM((ht, vs), bf16),
            pltpu.VMEM((N, NY, HZ, BLK, hs + ht), bf16),
            pltpu.VMEM((rows, (hs + ht) // 2), f32),
            pltpu.VMEM((rows, (hs + ht) // 2), f32),
            pltpu.VMEM((N, ROWS, vs), f32),
            pltpu.VMEM((N, ROWS, vs), f32),
            pltpu.VMEM((N, ROWS, vs), f32),
            pltpu.VMEM((2, N, ROWS, hs2), f32),
            pltpu.VMEM((2, N, ROWS, hs2), f32),
            pltpu.VMEM((N, ROWS, 128), f32),
            pltpu.VMEM((N, 8, ROWS), f32),
            pltpu.VMEM((N, 8, ROWS), f32),
            pltpu.VMEM((N, NZ, 8, ROWS), f32),
            pltpu.VMEM((N, 8, ROWS), f32),
            pltpu.VMEM((N, NY * NC, 8, ROWS), f32),
            pltpu.VMEM((N, ROWS, 128), f32),
            pltpu.VMEM((NY, HZ, N, BLK, 128), f32),
            pltpu.VMEM((N, ROWS, vs), bf16),
            pltpu.VMEM((N, ROWS, vs), bf16),
            pltpu.VMEM((N, ROWS, vs), bf16),
            pltpu.VMEM((N, ROWS, vs), bf16),
            pltpu.VMEM((N, NY, HZ, BLK, hs2), bf16),
            pltpu.VMEM((N, NY, HZ, BLK, ga), bf16),
            pltpu.VMEM((N, NC, HZ, BLK, ha), bf16),
            pltpu.VMEM((NC, NZ, BLK, ha), bf16),
            pltpu.VMEM((N, NZ, NY, BLK, gb), bf16),
            pltpu.VMEM((NC, NY, BLK, hb), bf16),
            pltpu.VMEM((NC, NY, BLK, hb), bf16),
            dma((2,)), dma(()), dma(()),
            dma((2,)), dma((N, 2, HZ)), dma((2,)), dma((N, 2)), dma((N, 2)), dma((N, 2)),
            dma((2,)), dma((2,)), dma((2,)), dma((2,)), dma((2, 2)),
            dma((2,)), dma((N, 2)),
            dma(()), dma((N,)), dma(()), dma((N,)), dma(()), dma(()), dma(()), dma((N,)),
            dma(()), dma(()), dma(()), dma((N,)),
            dma(()), dma((N,)), dma(()), dma(()),
            dma(()), dma(()), dma(()), dma(()),
        ],
        compiler_params=pltpu.CompilerParams(
            collective_id=0, has_side_effects=True, vmem_limit_bytes=60 * 1024 * 1024
        ),
        cost_estimate=pl.CostEstimate(
            flops=flops, bytes_accessed=2 * vs * (hs + ht), transcendentals=2 * tokens * vs
        ),
    )(
        student_hidden, teacher_hidden,
        segment_ids.reshape(1, tokens), valid_mask.reshape(1, tokens),
        student_head, teacher_head,
    )
    kl, grad = pl.pallas_call(
        split,
        out_shape=(jax.ShapeDtypeStruct((1, rows), f32), jax.ShapeDtypeStruct((rows, hs), bf16)),
        in_specs=[vmem],
        out_specs=(vmem, vmem),
    )(result)
    return kl.reshape(rows), grad


def solution(mesh):
    in_specs = (
        P(("dp", "vocab"), None),
        P(("dp", "vocab"), None),
        P("dp", "vocab"),
        P("dp", "vocab"),
        P("dp"),
        P("dp"),
    )
    out_specs = (P(("dp", "vocab")), P(("dp", "vocab"), None))
    return jax.shard_map(local, mesh=mesh, in_specs=in_specs, out_specs=out_specs, check_vma=False)
```
